32 devices in a mesh: bin: 4 (over y, x), grp: 8 (over z, core).
Axes of the slice: x: 2, y: 2, z: 4, core: 2. Of those that a mesh axis runs over, the one named last changes fastest.
Arguments:
- templates: bfloat16 [32768, 512], P(('bin', 'grp')), may hold values from -6 to 6
- owner_device: int32 [32768, 1], P(('bin', 'grp')), may hold values from 0 to 31; in each aligned block of 1024 rows (0 to 1023, 1024 to 2047, ...) at most 64 rows name the same one
- rate_code: int32 [32768], P(('bin', 'grp')), may hold values from 0 to 4
- rate_gains: float32 [5, 512], replicated, may hold values from 0.5 to 2
- sketch: float32 [512, 256], replicated, may hold values from -6 to 6
- strain: float32 [2, 65536], P(None, 'grp'), may hold values from -6 to 6
Outputs:
- mixing: bfloat16 [32768, 256], P(('bin', 'grp'))
- spectrum: float32 [4, 256], P('bin')
- filtered_0: bfloat16 [4, 2, 65536, 256], P('bin', None, 'grp')
- filtered_1: bfloat16 [4, 2, 32768, 256], P('bin', None, 'grp')
- filtered_2: bfloat16 [4, 2, 16384, 256], P('bin', None, 'grp')
- filtered_3: bfloat16 [4, 2, 8192, 256], P('bin', None, 'grp')
- filtered_4: bfloat16 [4, 2, 4096, 256], P('bin', None, 'grp')
The draws below stay inside these ranges and needn't reach their ends.
Inputs may be any that keep to these rules, and one draw needn't show every extreme that they name: `owner_device`: among the rows of one device, no device is named by more than 64 rows, and some device is named by exactly 64 rows.
All inputs are finite; a program needn't handle non-finite values.
Results may differ from the reference program's by a relative error of at most 0.0059.
Values may be sent and summed in bfloat16 or wider, within the bound.
No kernel may reach another device: no remote copies, remote signals or barrier semaphores. Data moves between devices by JAX's collectives and lax.ppermute only.
A program may use at most 128 MiB of HBM per device.

```python
import math
import jax
import jax.numpy as jnp
import numpy as np
from jax import lax

L = 512
K = 256
RATES = 5
DETECTORS = 2
TPL_DEV = 1024
TEMPLATES = 32768
CAP = 64
BINS = 4
BIN_ROWS = 8192
SAMPLES = 65536
N_GRP = 8
DEVICES = 32


def set_ends(array, rng, smallest, top_value):
    spot = [jax.random.randint(jax.random.fold_in(rng, axis), (), 0, length) for axis, length in enumerate(array.shape)]
    longest = array.shape.index(max(array.shape))
    next_to = spot[:longest] + [(spot[longest] + 1) % array.shape[longest]] + spot[longest + 1:]
    return array.at[tuple(spot)].set(smallest).at[tuple(next_to)].set(top_value)


def shard_levels(own_key, extent, split, least, high):
    factor_of = 1.0
    for axis_at, blocks in split:
        heights = jax.random.uniform(jax.random.fold_in(jax.random.fold_in(own_key, 6), axis_at), (blocks,), jnp.float32, least / len(split), high / len(split))
        factor_of = factor_of * jnp.repeat(jnp.exp(heights), extent[axis_at] // blocks).reshape((-1,) + (1,) * (len(extent) - 1 - axis_at))
    return factor_of


def assign_block(rng, own, number, rows, count, top, reach, lean):
    ranking = jax.random.permutation(rng, count)
    heavy_load, ordinary = shares(count, rows * top, reach, lean, True), shares(count, rows * top, reach, lean, False)
    places = jnp.arange(count)

    def named(tallies, rotation):
        used = int((tallies > 0).sum())
        fixed = max(1, used // 4)
        shifted = fixed + (places - fixed + rotation * (used - fixed)) % max(1, count - fixed)
        return jnp.zeros((count,), jnp.int32).at[ranking[jnp.where(places < fixed, places, shifted)]].set(jnp.asarray(tallies, jnp.int32))

    tallies = jnp.where(number % 4 == 0, named(heavy_load, number // 4), named(ordinary, number - number // 4 - 1))
    mixed = jax.random.permutation(jax.random.fold_in(own, 3), count)
    source_of, receiver = mixed[0:count // 2 * 2:2], mixed[1:count // 2 * 2:2]
    margin = jnp.minimum(tallies[source_of] - 1, reach - tallies[receiver]) // 2
    margin = jnp.where((source_of == ranking[0]) | (receiver == ranking[0]) | (tallies[receiver] == 0), 0, jnp.maximum(margin, 0))
    shifted = jax.random.randint(jax.random.fold_in(own, 4), (count // 2,), 0, 1 << 20) % (margin + 1)
    tallies = tallies.at[source_of].add(-shifted).at[receiver].add(shifted)
    items = jnp.searchsorted(jnp.cumsum(tallies), jnp.arange(rows * top), side="right").astype(jnp.int32)
    table = items.reshape(top, rows).T
    table = table[jax.random.permutation(jax.random.fold_in(own, 1), rows)]
    rotation = jax.random.randint(jax.random.fold_in(own, 2), (rows, 1), 0, top)
    return jnp.take_along_axis(table, (jnp.arange(top)[None, :] + rotation) % top, axis=1)


def shares(count, total, most, slope, full):
    loads = [(1 << 20) // math.isqrt(grade ** slope) + 1 for grade in range(1, count + 1)]
    largest = most if full else min(most, max(-(-total // count), total * loads[0] // sum(loads)))
    least = 1 if total - largest >= count - 1 else 0
    holding, spare = [largest] + [least] * (count - 1), total - largest - least * (count - 1)
    while spare > 0:
        movable = [i for i in range(1, count) if holding[i] < largest] or [i for i in range(1, count) if holding[i] < most]
        mass, remaining = sum([loads[i] for i in movable]), spare
        for i in movable:
            more = min(most - holding[i], max(1, remaining * loads[i] // mass), spare)
            holding[i] = holding[i] + more
            spare = spare - more
    return np.array(holding)


def scatter_about(rng, shape, width, most, cuts=(), kind=jnp.bfloat16):
    result = width * jax.random.normal(rng, shape, jnp.float32)
    if cuts:
        result = result * shard_levels(rng, shape, cuts, -0.22, 0.18)
    return jnp.clip(result, -most, most).astype(kind)


def setup_inputs(seed: int = 0) -> dict:
    splits = jax.random.split(jax.random.key(seed), 7)
    templates = scatter_about(splits[0], (TEMPLATES, L), 1.0, 6.0, ((0, 32),))
    owner_device_keys = jax.random.split(jax.random.fold_in(splits[1], 1), TEMPLATES // TPL_DEV)
    owner_device_turns = jax.random.permutation(jax.random.fold_in(splits[1], 3), TEMPLATES // TPL_DEV)
    owner_device = jax.vmap(lambda own, number: assign_block(jax.random.fold_in(splits[1], 2), own, number, TPL_DEV, DEVICES, 1, CAP, 2))(owner_device_keys, owner_device_turns).reshape((TEMPLATES, 1))
    rate_code = set_ends(jax.random.randint(splits[2], (TEMPLATES,), 0, RATES), jax.random.fold_in(splits[2], 1), 0, RATES - 1).astype(jnp.int32)
    rate_gains = jnp.clip(jnp.exp(jax.random.uniform(splits[3], (RATES, L), jnp.float32, math.log(0.5), math.log(2.0))), 0.5, 2.0)
    sketch = scatter_about(splits[4], (L, K), 1.0, 6.0, (), jnp.float32)
    strain = scatter_about(splits[5], (DETECTORS, SAMPLES), 1.0, 6.0, ((1, 8),), jnp.float32)
    return dict(templates=templates, owner_device=owner_device, rate_code=rate_code, rate_gains=rate_gains, sketch=sketch, strain=strain)


highest = lax.Precision.HIGHEST
inv_root_two = 0.7071067811865476

def whiten_rows(templates, rate_code, rate_gains):
    factor = jnp.zeros(templates.shape, jnp.float32)
    for rate_level in range(rate_gains.shape[0]):
        factor = factor + jnp.where((rate_code == rate_level)[:, None], rate_gains[rate_level][None, :], jnp.float32(0.0))
    return (templates.astype(jnp.float32) * factor).astype(jnp.bfloat16)

def reference(templates, owner_device, rate_code, rate_gains, sketch, strain):
    whitened = whiten_rows(templates, rate_code, rate_gains)
    wide_rows = whitened.astype(jnp.float32)
    bin_of_row = owner_device[:, 0] // N_GRP
    spectra = []
    bases = []
    mixing = jnp.zeros((wide_rows.shape[0], K), jnp.float32)
    for bin_number in range(BINS):
        member = bin_of_row == bin_number
        masked = jnp.where(member[:, None], wide_rows, jnp.float32(0.0))
        gram_total = lax.dot_general(masked, wide_rows, (((0,), (0,)), ((), ())), precision=highest)
        product = jnp.dot(gram_total, sketch, precision=highest)
        inner_gram = jnp.dot(product.T, product, precision=highest)
        lower_factor = jnp.linalg.cholesky(inner_gram)
        spectra.append(jnp.diagonal(lower_factor) / (BIN_ROWS * math.sqrt(L)))
        basis_bf = jax.scipy.linalg.solve_triangular(lower_factor, product.T, lower=True).T.astype(jnp.bfloat16)
        bases.append(basis_bf)
        coeffs = jnp.dot(wide_rows, basis_bf.astype(jnp.float32), precision=highest)
        mixing = mixing + jnp.where(member[:, None], coeffs, jnp.float32(0.0))
    outputs = [mixing.astype(jnp.bfloat16), jnp.stack(spectra)]
    current = strain
    for rate_level in range(RATES):
        if rate_level > 0:
            paired = current.reshape(current.shape[0], -1, 2)
            current = (paired[:, :, 0] + paired[:, :, 1]) * inv_root_two
        rounded = lax.optimization_barrier(current.astype(jnp.bfloat16)).astype(jnp.float32)
        stride = 2 ** rate_level
        per_bin = []
        for bin_number in range(BINS):
            tap_rows = bases[bin_number][::stride].astype(jnp.float32)
            tap_count = tap_rows.shape[0]
            result_level = lax.conv_general_dilated(rounded[:, :, None], tap_rows[::-1][:, None, :], (1,), [(tap_count - 1, 0)], dimension_numbers=('NWC', 'WIO', 'NWC'), precision=highest)
            per_bin.append(result_level.astype(jnp.bfloat16))
        outputs.append(jnp.stack(per_bin))
    return (outputs[0], outputs[1], outputs[2], outputs[3], outputs[4], outputs[5], outputs[6])
```

```python
import functools
import math

import jax
import jax.numpy as jnp
from jax import lax
from jax.experimental import pallas as pl
from jax.experimental.pallas import tpu as pltpu
from jax.sharding import PartitionSpec as P

highest = lax.Precision.HIGHEST
inv_root_two = 0.7071067811865476
f32 = jnp.float32
bf16 = jnp.bfloat16
LANES = 128
BLOCK = 32
VMEM_BYTES = 60 * 1024 * 1024


def iota(shape, axis):
    return lax.broadcasted_iota(jnp.int32, shape, axis)


def split3(x):
    high = x.astype(bf16)
    rest = x - high.astype(f32)
    middle = rest.astype(bf16)
    low = (rest - middle.astype(f32)).astype(bf16)
    return high, middle, low


def dot(a, b, precision=None):
    return jnp.dot(a, b, preferred_element_type=f32, precision=precision)


def dot_t(a, b, precision=None):
    return lax.dot_general(
        a, b, (((0,), (0,)), ((), ())), preferred_element_type=f32, precision=precision
    )


def params(**kw):
    return pltpu.CompilerParams(vmem_limit_bytes=VMEM_BYTES, **kw)


def spread(group, rows, groups, width):
    member = (iota((8, rows), 0) == group).astype(f32).astype(bf16)
    column = (iota((8, groups * width), 0) == iota((8, groups * width), 1) // width).astype(f32)
    return dot_t(member, column.astype(bf16))


def front_body(bins, grp, place_ref, owner_ref, code_ref, gains_ref, templates_ref, sketch_ref,
               white_ref, keep_ref, send_ref, product_ref):
    rows, width = templates_ref.shape
    rank = sketch_ref.shape[1]
    rates = gains_ref.shape[0]
    gains = jnp.concatenate([gains_ref[...], jnp.zeros((8 - rates, width), f32)], axis=0)
    member = (iota((8, rows), 0) == code_ref[...]).astype(f32)
    member = jnp.concatenate([member, member, member], axis=0).astype(bf16)
    parts = jnp.concatenate([part.astype(f32) for part in split3(gains)], axis=0).astype(bf16)
    factor = dot_t(member, parts)
    white = (templates_ref[...].astype(f32) * factor).astype(bf16)
    white_ref[...] = white
    sketched = None
    for part in split3(sketch_ref[...]):
        term = dot(white, part)
        sketched = term if sketched is None else sketched + term
    mask = spread(owner_ref[...] // grp, rows, bins, rank).astype(bf16)
    total = None
    for part in split3(sketched):
        term = dot_t(white, jnp.concatenate([part] * bins, axis=1) * mask)
        total = term if total is None else total + term
    product_ref[...] = total
    half = width // 2
    core = place_ref[0]
    for b in range(bins):
        columns = slice(b * rank, (b + 1) * rank)
        keep_ref[b] = product_ref[pl.ds(pl.multiple_of(core * half, half), half), columns]
        send_ref[b] = product_ref[pl.ds(pl.multiple_of((1 - core) * half, half), half), columns]


def front(place, owner, code, gains, templates, sketch, bins, grp):
    rows, width = templates.shape
    rank = sketch.shape[1]
    half = jax.ShapeDtypeStruct((bins, width // 2, rank), f32)
    vmem = pl.BlockSpec(memory_space=pltpu.VMEM)
    return pl.pallas_call(
        functools.partial(front_body, bins, grp),
        out_shape=(jax.ShapeDtypeStruct((rows, width), bf16), half, half),
        in_specs=[pl.BlockSpec(memory_space=pltpu.SMEM)] + [vmem] * 5,
        out_specs=(vmem, vmem, vmem),
        scratch_shapes=[pltpu.VMEM((width, bins * rank), f32)],
        compiler_params=params(),
        name="whiten_product",
    )(place, owner, code, gains, templates, sketch)


def pick(x, index):
    return lax.dynamic_index_in_dim(x, index, 0, keepdims=False)


def flip_bin(x, bit, bins):
    return lax.ppermute(x, "bin", [(i, i ^ bit) for i in range(bins)])


def flip_grp(x, bit, grp):
    return lax.ppermute(x, "grp", [(i, i ^ bit) for i in range(grp)])


def reduce_products(keep, send, bins, grp):
    total = keep + flip_grp(send, 1, grp)
    rows = total.shape[1]
    here = lax.axis_index("bin")
    high, low = here >> 1, here & 1

    def by(x, bit):
        x = x.reshape((2, 2) + x.shape[1:])
        return x if bit else jnp.swapaxes(x, 0, 1)

    first = by(total[:, : rows // 2], 0)
    second = by(total[:, rows // 2 :], 1)
    first = pick(first, low) + flip_bin(pick(first, 1 - low), 1, bins)
    second = pick(second, high) + flip_bin(pick(second, 1 - high), 2, bins)
    first = pick(first, high) + flip_bin(pick(first, 1 - high), 2, bins)
    second = pick(second, low) + flip_bin(pick(second, 1 - low), 1, bins)
    mine = jnp.concatenate([first, second], axis=0)
    chips = grp // 2
    chip = lax.axis_index("grp") // 2
    shares = mine.reshape((chips, rows // chips) + mine.shape[1:])
    share = pick(shares, chip)
    for d in range(1, chips):
        share = share + flip_grp(pick(shares, chip ^ d), 2 * d, grp)
    pieces = jnp.stack([share] + [flip_grp(share, 2 * d, grp) for d in range(1, chips)])
    other = flip_grp(pieces, 1, grp)
    return pieces, other


def basis_body(place_ref, mine_ref, other_ref, taps_ref, diag_ref, product_ref, work_ref, wide_ref):
    chips, share, rank = mine_ref.shape
    length = 2 * chips * share
    half = length // 2
    core, chip = place_ref[0], place_ref[1]
    for d in range(chips):
        row = (chip ^ d) * share
        product_ref[pl.ds(pl.multiple_of(core * half + row, share), share), :] = mine_ref[d]
        product_ref[pl.ds(pl.multiple_of((1 - core) * half + row, share), share), :] = other_ref[d]
    product = product_ref[...]
    product_t = product.T
    work_ref[:, :rank] = dot(product_t, product, highest)
    work_ref[:, rank:] = product_t
    lane = iota((BLOCK, LANES), 1)
    row_at = iota((BLOCK, LANES), 0)
    per_tile = LANES // BLOCK
    for j in range(rank // BLOCK):
        rows = slice(j * BLOCK, (j + 1) * BLOCK)
        offset = (j % per_tile) * BLOCK
        eye_at = ((j + 1) % per_tile) * BLOCK
        tile_at = (j // per_tile) * LANES
        tile = work_ref[rows, tile_at : tile_at + LANES]
        state = jnp.where(
            (lane >= offset) & (lane < offset + BLOCK),
            tile,
            jnp.where(lane == row_at + eye_at, f32(1.0), f32(0.0)),
        )
        for k in range(BLOCK):
            column = jnp.broadcast_to(state[:, offset + k : offset + k + 1], (BLOCK, LANES))
            scale = 1.0 / column[k : k + 1, :]
            state = state - jnp.where(row_at > k, column, f32(0.0)) * (state[k : k + 1, :] * scale)
        pivot = jnp.sum(jnp.where(lane == row_at + offset, state, f32(0.0)), axis=1, keepdims=True)
        inverse = state[:, eye_at : eye_at + BLOCK] * lax.rsqrt(pivot)
        solved = dot(inverse, work_ref[rows, :], highest)
        work_ref[rows, :] = solved
        after = (j + 1) * BLOCK
        if after < rank:
            change = dot_t(solved[:, :rank], solved, highest)
            work_ref[after:, :] = work_ref[after:, :] - change[after:, :]
    on_diagonal = iota((rank, rank), 0) == iota((rank, rank), 1)
    diag_ref[...] = jnp.sum(
        jnp.where(on_diagonal, work_ref[:, :rank], f32(0.0)), axis=0, keepdims=True
    )
    basis = work_ref[:, rank:].T
    for part in range(rank // LANES):
        wide_ref[part] = basis[:, part * LANES : (part + 1) * LANES]
    at = 0
    taps, level = length, 0
    while at < taps_ref.shape[0]:
        rows = max(taps, LANES)
        chosen = jnp.concatenate(
            [wide_ref[part, pl.ds(0, taps, stride=2**level), :] for part in range(rank // LANES)],
            axis=1,
        )
        if rows > taps:
            chosen = jnp.concatenate([chosen, jnp.zeros((rows - taps, rank), f32)], axis=0)
        taps_ref[at : at + rows, :] = chosen.astype(bf16)
        at, taps, level = at + rows, taps // 2, level + 1


def find_basis(place, mine, other, tap_rows):
    chips, share, rank = mine.shape
    length = 2 * chips * share
    vmem = pl.BlockSpec(memory_space=pltpu.VMEM)
    return pl.pallas_call(
        basis_body,
        out_shape=(
            jax.ShapeDtypeStruct((tap_rows, rank), bf16),
            jax.ShapeDtypeStruct((1, rank), f32),
        ),
        in_specs=[pl.BlockSpec(memory_space=pltpu.SMEM), vmem, vmem],
        out_specs=(vmem, vmem),
        scratch_shapes=[
            pltpu.VMEM((length, rank), f32),
            pltpu.VMEM((rank, rank + length), f32),
            pltpu.VMEM((rank // LANES, length, LANES), f32),
        ],
        compiler_params=params(),
        name="cholesky_basis",
    )(place, mine, other)


def level_sizes(levels, tap_count):
    return [max(1, (tap_count >> r) // LANES) for r in range(levels)]


def tiles_body(levels, blocks, detectors, chunks, strain_ref, tiles_ref, level_ref, flipped_ref):
    step = pl.program_id(0)
    total = strain_ref.shape[0]
    starts = [0]
    for r in range(levels):
        starts.append(starts[-1] + (total >> r))

    @pl.when(step == 0)
    def _():
        source = iota((2 * LANES, 2 * LANES), 0)
        target = iota((2 * LANES, 2 * LANES), 1)
        even_odd = (source == 2 * (target % LANES) + target // LANES).astype(f32).astype(bf16)
        reverse = (
            iota((LANES, LANES), 0) + iota((LANES, LANES), 1) == LANES - 1
        ).astype(f32).astype(bf16)
        level_ref[: total, :] = strain_ref[...]
        for r in range(levels):
            rows = total >> r
            at = starts[r]
            if r > 0:
                before = starts[r - 1]
                joined = jnp.concatenate(
                    [
                        level_ref[pl.ds(before, rows, stride=2), :],
                        level_ref[pl.ds(before + 1, rows, stride=2), :],
                    ],
                    axis=1,
                )
                high, middle, low = split3(joined)
                both = (dot(high, even_odd) + dot(middle, even_odd)) + dot(low, even_odd)
                level_ref[at : at + rows, :] = (both[:, :LANES] + both[:, LANES:]) * inv_root_two
            flipped_ref[at : at + rows, :] = dot(level_ref[at : at + rows, :].astype(bf16), reverse)

    detector = step // chunks
    chunk = step % chunks
    lower = iota((LANES, LANES), 1) <= iota((LANES, LANES), 0)
    at = 0
    for r in range(levels):
        rows = (total >> r) // detectors
        history = (1 << (levels - 1)) >> r
        count = (rows - history) // chunks
        first = starts[r] + detector * rows + history + chunk * count - (blocks[r] - 1)

        def turned(row):
            line = jnp.broadcast_to(flipped_ref[pl.ds(row, 1), :], (LANES, LANES))
            return pltpu.roll(line, 1, 1, stride=1, stride_axis=0)

        before = turned(first - 1)
        for i in range(count + blocks[r] - 1):
            now = turned(first + i)
            tiles_ref[0, at] = jnp.where(lower, now, before).astype(bf16)
            before = now
            at += 1


def make_tiles(strain_rows, levels, blocks, detectors, chunks):
    total = strain_rows.shape[0]
    count = 0
    for r in range(levels):
        rows = (total >> r) // detectors
        history = (1 << (levels - 1)) >> r
        count += (rows - history) // chunks + blocks[r] - 1
    steps = detectors * chunks
    held = sum(total >> r for r in range(levels))
    held = -(-held // 8) * 8
    return pl.pallas_call(
        functools.partial(tiles_body, levels, blocks, detectors, chunks),
        grid=(steps,),
        out_shape=jax.ShapeDtypeStruct((steps, count, LANES, LANES), bf16),
        in_specs=[pl.BlockSpec((total, LANES), lambda i: (0, 0))],
        out_specs=pl.BlockSpec((1, count, LANES, LANES), lambda i: (i, 0, 0, 0)),
        scratch_shapes=[pltpu.VMEM((held, LANES), f32), pltpu.VMEM((held, LANES), f32)],
        compiler_params=params(),
        cost_estimate=pl.CostEstimate(
            flops=steps * count * LANES * LANES * 64, bytes_accessed=steps * count * LANES * LANES * 2,
            transcendentals=0,
        ),
        name="toeplitz_tiles",
    )(strain_rows)


def filter_body(blocks, tiles_ref, taps_ref, *out_refs):
    at, tap_at = 0, 0
    for r, out_ref in enumerate(out_refs):
        count = out_ref.shape[2] // LANES
        b = blocks[r]
        taps = taps_ref[tap_at : tap_at + b * LANES, :]
        group = min(count, 4)
        for i in range(0, count, group):
            columns = [
                tiles_ref[0, at + b - 1 - k + i : at + b - 1 - k + i + group].reshape(
                    group * LANES, LANES
                )
                for k in range(b)
            ]
            joined = jnp.concatenate(columns, axis=1) if b > 1 else columns[0]
            out_ref[0, 0, i * LANES : (i + group) * LANES, :] = dot(joined, taps).astype(bf16)
        at += count + b - 1
        tap_at += b * LANES


def filter_levels(tiles, taps, lengths, blocks, detectors, chunks):
    rank = taps.shape[1]
    steps, count = tiles.shape[:2]
    out_shape = [jax.ShapeDtypeStruct((1, detectors, n, rank), bf16) for n in lengths]
    return pl.pallas_call(
        functools.partial(filter_body, blocks),
        grid=(steps,),
        out_shape=out_shape,
        in_specs=[
            pl.BlockSpec((1, count, LANES, LANES), lambda i: (i, 0, 0, 0)),
            pl.BlockSpec(taps.shape, lambda i: (0, 0)),
        ],
        out_specs=[
            pl.BlockSpec((1, 1, n // chunks, rank), lambda i: (0, i // chunks, i % chunks, 0))
            for n in lengths
        ],
        compiler_params=params(),
        cost_estimate=pl.CostEstimate(
            flops=8 * sum(lengths) * LANES * rank * detectors,
            bytes_accessed=2 * detectors * sum(lengths) * rank + 2 * math.prod(tiles.shape),
            transcendentals=0,
        ),
        name="filter_levels",
    )(tiles, taps)


def mixing_body(bins, grp, place_ref, owner_ref, white_ref, own_ref, mine_ref, other_ref, out_ref,
                bases_ref):
    rows, width = white_ref.shape
    rank = own_ref.shape[1]
    half = width // 2
    core, here = place_ref[0], place_ref[2]
    bases_ref[0] = own_ref[...]
    for m in range(1, bins):
        bases_ref[m, pl.ds(pl.multiple_of(core * half, half), half), :] = mine_ref[m - 1]
        bases_ref[m, pl.ds(pl.multiple_of((1 - core) * half, half), half), :] = other_ref[m - 1]
    mask = spread((owner_ref[...] // grp) ^ here, rows, bins, rank)
    white = white_ref[...]
    total = None
    for m in range(bins):
        chosen = mask[:, m * rank : (m + 1) * rank] > 0.5
        term = jnp.where(chosen, dot(white, bases_ref[m]), f32(0.0))
        total = term if total is None else total + term
    out_ref[...] = total.astype(bf16)


def mix(place, owner, white, own, mine, other, grp):
    rows, width = white.shape
    rank = own.shape[1]
    bins = mine.shape[0] + 1
    vmem = pl.BlockSpec(memory_space=pltpu.VMEM)
    return pl.pallas_call(
        functools.partial(mixing_body, bins, grp),
        out_shape=jax.ShapeDtypeStruct((rows, rank), bf16),
        in_specs=[pl.BlockSpec(memory_space=pltpu.SMEM)] + [vmem] * 5,
        out_specs=vmem,
        scratch_shapes=[pltpu.VMEM((bins, width, rank), bf16)],
        compiler_params=params(),
        name="mixing",
    )(place, owner, white, own, mine, other)


def local(templates, owner_device, rate_code, rate_gains, sketch, strain):
    rows, width = templates.shape
    grp = lax.axis_size("grp")
    bins = lax.axis_size("bin")
    levels = rate_gains.shape[0]
    detectors, samples = strain.shape
    here, spot = lax.axis_index("bin"), lax.axis_index("grp")
    place = jnp.stack([spot % 2, spot // 2, here]).astype(jnp.int32)
    owner = owner_device.reshape(1, rows)

    white, keep, send = front(
        place, owner, rate_code.reshape(1, rows), rate_gains, templates, sketch, bins, grp
    )

    reach = LANES << (levels - 1)
    history = lax.ppermute(strain[:, -reach:], "grp", [(i, i + 1) for i in range(grp - 1)])
    strain_rows = jnp.concatenate([history, strain], axis=1).reshape(-1, LANES)
    blocks = level_sizes(levels, width)
    chunks = 4
    tiles = make_tiles(strain_rows, levels, blocks, detectors, chunks)

    mine, other = reduce_products(keep, send, bins, grp)
    taps, diag = find_basis(place, mine, other, sum(blocks) * LANES)
    own = taps[:width]
    part = lax.dynamic_slice_in_dim(own, (spot % 2) * (width // 2), width // 2, 0)
    theirs = jnp.stack([flip_bin(part, m, bins) for m in range(1, bins)])
    theirs_other = flip_grp(theirs, 1, grp)
    lengths = [samples >> r for r in range(levels)]
    filtered = filter_levels(tiles, taps, lengths, blocks, detectors, chunks)
    mixing = mix(place, owner, white, own, theirs, theirs_other, grp)
    spectrum = diag / (rows * grp * math.sqrt(width))
    return (mixing, spectrum, *filtered)


def solution(mesh):
    return jax.shard_map(
        local,
        mesh=mesh,
        in_specs=(
            P(("bin", "grp"), None),
            P(("bin", "grp"), None),
            P(("bin", "grp")),
            P(),
            P(),
            P(None, "grp"),
        ),
        out_specs=(
            P(("bin", "grp"), None),
            P("bin", None),
            P("bin", None, "grp", None),
            P("bin", None, "grp", None),
            P("bin", None, "grp", None),
            P("bin", None, "grp", None),
            P("bin", None, "grp", None),
        ),
        check_vma=False,
    )
```

```python
import functools
import math

import jax
import jax.numpy as jnp
from jax import lax
from jax.experimental import pallas as pl
from jax.experimental.pallas import tpu as pltpu
from jax.sharding import PartitionSpec as P

highest = lax.Precision.HIGHEST
inv_root_two = 0.7071067811865476
f32 = jnp.float32
bf16 = jnp.bfloat16
LANES = 128
SUBLANES = 8
MIB = 1024 * 1024


def iota(shape, axis):
    return lax.broadcasted_iota(jnp.int32, shape, axis)


def split3(x):
    high = x.astype(bf16)
    rest = x - high.astype(f32)
    middle = rest.astype(bf16)
    low = (rest - middle.astype(f32)).astype(bf16)
    return high, middle, low


def split2(x):
    high = x.astype(bf16)
    return high, (x - high.astype(f32)).astype(bf16)


def dot(a, b, precision=None):
    return jnp.dot(a, b, preferred_element_type=f32, precision=precision)


def dot_t(a, b, precision=None):
    return lax.dot_general(
        a, b, (((0,), (0,)), ((), ())), preferred_element_type=f32, precision=precision
    )


def params(mib):
    return pltpu.CompilerParams(vmem_limit_bytes=mib * MIB)


def spread(group, rows, groups, width):
    member = (iota((8, rows), 0) == group).astype(f32).astype(bf16)
    column = (iota((8, groups * width), 0) == iota((8, groups * width), 1) // width).astype(f32)
    return dot_t(member, column.astype(bf16))


def front_body(bins, grp, owner_ref, code_ref, gains_hbm, templates_hbm, sketch_hbm, white_hbm, keep_hbm,
               send_hbm, gains_ref, templates_ref, sketch_ref, white_ref, sketched_ref, keep_ref, send_ref,
               sem, out_sem):
    rows, width = templates_ref.shape
    rates = gains_ref.shape[0]
    pieces = 4
    piece = rows // pieces
    copies = [
        pltpu.make_async_copy(gains_hbm, gains_ref, sem.at[0]),
        pltpu.make_async_copy(sketch_hbm, sketch_ref, sem.at[1]),
    ]
    for i in range(pieces):
        at = pl.ds(i * piece, piece)
        copies.append(
            pltpu.make_async_copy(templates_hbm.at[at], templates_ref.at[at], sem.at[2 + i])
        )
    for copy in copies:
        copy.start()
    given = [
        pltpu.make_async_copy(white_ref, white_hbm, out_sem.at[0]),
        pltpu.make_async_copy(send_ref, send_hbm, out_sem.at[1]),
        pltpu.make_async_copy(keep_ref, keep_hbm, out_sem.at[2]),
    ]
    member = (iota((8, rows), 0) == code_ref[...]).astype(f32)
    member = jnp.concatenate([member, member, member], axis=0).astype(bf16)
    mask = spread(owner_ref[...] // grp, rows, bins, LANES).astype(bf16)
    copies[0].wait()
    gains = jnp.concatenate([gains_ref[...], jnp.zeros((8 - rates, width), f32)], axis=0)
    parts = jnp.concatenate([part.astype(f32) for part in split3(gains)], axis=0).astype(bf16)
    copies[1].wait()
    sketch_parts = split2(sketch_ref[...])
    for i in range(pieces):
        at = slice(i * piece, (i + 1) * piece)
        factor = dot_t(member[:, at], parts)
        copies[2 + i].wait()
        white = (templates_ref[at, :].astype(f32) * factor).astype(bf16)
        white_ref[at, :] = white
        sketched = None
        for part in sketch_parts:
            term = dot(white, part)
            sketched = term if sketched is None else sketched + term
        sketched_ref[at, :] = sketched
    given[0].start()
    core = lax.axis_index("grp") % 2
    sketched_parts = split2(sketched_ref[...])
    products(bins, 1 - core, mask, white_ref, sketched_parts, send_ref)
    given[1].start()
    products(bins, core, mask, white_ref, sketched_parts, keep_ref)
    given[2].start()
    for copy in given:
        copy.wait()


def products(bins, which, mask, white_ref, sketched_parts, out_ref):
    rows, width = white_ref.shape
    half = width // 2
    chosen = white_ref[:, pl.ds(pl.multiple_of(which * half, half), half)]
    masked = jnp.concatenate(
        [
            chosen * jnp.concatenate([mask[:, b * LANES : (b + 1) * LANES]] * (half // LANES), axis=1)
            for b in range(bins)
        ],
        axis=1,
    )
    total = None
    for part in sketched_parts:
        term = dot_t(masked, part)
        total = term if total is None else total + term
    for b in range(bins):
        high, low = b // 2, b % 2
        one, two = jnp.where(which == 0, low, high), jnp.where(which == 0, high, low)
        for i in range(out_ref.shape[0]):
            out_ref[i, one, two] = total[b * half : (b + 1) * half, i * LANES : (i + 1) * LANES]


def halves(bins, width, rank):
    return (rank // LANES, 2, bins // 2, width // 2, LANES)


def front(owner, code, gains, templates, sketch, bins, grp):
    rows, width = templates.shape
    rank = sketch.shape[1]
    vmem, anywhere = pl.BlockSpec(memory_space=pltpu.VMEM), pl.BlockSpec(memory_space=pl.ANY)
    sent = halves(bins, width, rank)
    return pl.pallas_call(
        functools.partial(front_body, bins, grp),
        out_shape=(
            jax.ShapeDtypeStruct((rows, width), bf16),
            jax.ShapeDtypeStruct(sent, f32),
            jax.ShapeDtypeStruct(sent, f32),
        ),
        in_specs=[vmem, vmem, anywhere, anywhere, anywhere],
        out_specs=(anywhere, anywhere, anywhere),
        scratch_shapes=[
            pltpu.VMEM(gains.shape, f32),
            pltpu.VMEM(templates.shape, bf16),
            pltpu.VMEM(sketch.shape, f32),
            pltpu.VMEM((rows, width), bf16),
            pltpu.VMEM((rows, rank), f32),
            pltpu.VMEM(sent, f32),
            pltpu.VMEM(sent, f32),
            pltpu.SemaphoreType.DMA((6,)),
            pltpu.SemaphoreType.DMA((3,)),
        ],
        compiler_params=params(60),
        name="whiten_products",
    )(owner, code, gains, templates, sketch)


def pick(x, index):
    return lax.dynamic_index_in_dim(x, index, 0, keepdims=False)


def flip_bin(x, bits, bins, grp):
    pairs = [
        (b * grp + g, (b ^ bits[g % 2]) * grp + g) for b in range(bins) for g in range(grp)
    ]
    return lax.ppermute(x, ("bin", "grp"), pairs)


def flip_core(x, grp):
    return lax.ppermute(x, "grp", [(i, i ^ 1) for i in range(grp)])


def flip_chip(x, bits, grp):
    return lax.ppermute(x, "grp", [(i, i ^ (2 * bits[i % 2])) for i in range(grp)])


def reduce_products(keep, send, bins, grp, beside):
    keep, done = beside[0](keep, ())
    came = flip_core(send, grp)
    came, *done = lax.optimization_barrier((came, *done))
    came, done = beside[1](came, done)
    here = lax.axis_index("bin")
    core = lax.axis_index("grp") % 2
    high, low = here >> 1, here & 1
    one, two = jnp.where(core == 0, low, high), jnp.where(core == 0, high, low)
    pieces = range(keep.shape[0])

    def stage(held, leaving, move):
        arrived = [move(x) for x in leaving]
        return [x + y for x, y in zip(held, arrived)]

    total = stage(
        [pick(keep[i], one) + pick(came[i], one) for i in pieces],
        [pick(keep[i], 1 - one) + pick(came[i], 1 - one) for i in pieces],
        lambda x: flip_bin(x, (1, 2), bins, grp),
    )
    *total, done_0, done_1 = lax.optimization_barrier((*total, *done))
    total[-1], done = beside[2](total[-1], (done_0, done_1))
    mine = stage(
        [pick(x, two) for x in total],
        [pick(x, 1 - two) for x in total],
        lambda x: flip_bin(x, (2, 1), bins, grp),
    )
    bits = [1 << i for i in range((grp // 2).bit_length() - 1)]
    mine[-1], *done = lax.optimization_barrier((mine[-1], *done))
    for step, bit in enumerate(bits):
        mine = stage(mine, mine, lambda x: flip_chip(x, (bit, bits[-1 - step]), grp))
    return mine, [flip_core(x, grp) for x in mine], done


def eliminate(state):
    finished = []
    size = state.shape[0]
    head = iota((SUBLANES, size), 0)
    for start in range(0, size, SUBLANES):
        lane = iota(state.shape, 1)
        columns = [
            jnp.broadcast_to(state[:, start + k : start + k + 1], state.shape)
            for k in range(SUBLANES)
        ]
        state = jnp.where((lane >= start) & (lane < start + SUBLANES), f32(0.0), state)
        eye = iota((SUBLANES, size), 1) == head + start
        top = jnp.where(eye, f32(1.0), state[:SUBLANES])
        rest = state[SUBLANES:]
        more = rest.shape[0] > 0
        tops = [column[:SUBLANES] for column in columns]
        rests = [column[SUBLANES:] for column in columns]
        pivots = jnp.zeros((SUBLANES, size), f32)
        for k in range(SUBLANES):
            pivot = tops[k][k : k + 1]
            inverse = 1.0 / pivot
            below = jnp.where(head > k, tops[k], f32(0.0))
            factor = rests[k] * inverse if more else None
            for j in range(k + 1, SUBLANES):
                across = tops[j][k : k + 1]
                tops[j] = tops[j] - (below * across) * inverse
                if more:
                    rests[j] = rests[j] - factor * across
            across = top[k : k + 1]
            top = top - (below * across) * inverse
            if more:
                rest = rest - factor * across
            pivots = jnp.where(head == k, pivot, pivots)
        finished.append(top * lax.rsqrt(pivots))
        state = rest
    inverse = jnp.concatenate(finished, axis=0)
    return jnp.where(iota((size, size), 0) >= iota((size, size), 1), inverse, f32(0.0))


def joined_rows(mine_ref, other_ref, product_ref):
    half = mine_ref.shape[0]
    core = lax.axis_index("grp") % 2
    product_ref[pl.ds(pl.multiple_of(core * half, half), half), :] = mine_ref[...]
    product_ref[pl.ds(pl.multiple_of((1 - core) * half, half), half), :] = other_ref[...]
    return product_ref[...]


def basis_piece(scale_down, product, before):
    inner = dot_t(product, product, highest)
    rest = product
    for basis in before:
        across = dot_t(basis, product, highest)
        inner = inner - dot_t(across, across, highest)
        rest = rest - dot(basis, across, highest)
    inverse = eliminate(inner)
    basis = lax.dot_general(
        rest, inverse, (((1,), (1,)), ((), ())), preferred_element_type=f32, precision=highest
    )
    eye = iota(inverse.shape, 0) == iota(inverse.shape, 1)
    diagonal = jnp.sum(jnp.where(eye, inverse, f32(0.0)), axis=0, keepdims=True)
    return basis, (1.0 / diagonal) / scale_down


def piece_body(scale_down, mine_ref, other_ref, basis_ref, spectrum_ref, product_ref):
    product = joined_rows(mine_ref, other_ref, product_ref)
    basis_ref[...], spectrum_ref[...] = basis_piece(scale_down, product, [])


def first_piece(mine, other, scale_down):
    half, columns = mine.shape
    return pl.pallas_call(
        functools.partial(piece_body, scale_down),
        out_shape=(
            jax.ShapeDtypeStruct((2 * half, columns), f32),
            jax.ShapeDtypeStruct((1, columns), f32),
        ),
        scratch_shapes=[pltpu.VMEM((2 * half, columns), f32)],
        compiler_params=params(8),
        name="basis_first",
    )(mine, other)


def basis_body(scale_down, first_ref, first_spectrum_ref, mine_ref, other_ref, own_ref, part_ref, taps_ref,
               spectrum_ref, product_ref, wide_ref):
    half = mine_ref.shape[0]
    core = lax.axis_index("grp") % 2
    product = joined_rows(mine_ref, other_ref, product_ref)
    first = first_ref[...]
    wide_ref[0] = first
    wide_ref[1], spectrum_ref[:, LANES:] = basis_piece(scale_down, product, [first])
    spectrum_ref[:, :LANES] = first_spectrum_ref[...]
    own_ref[...] = jnp.concatenate([wide_ref[0], wide_ref[1]], axis=1).astype(bf16)
    part_ref[...] = own_ref[pl.ds(pl.multiple_of(core * half, half), half), :]
    at = 0
    taps, level = half, 1
    while at < taps_ref.shape[0]:
        rows = max(taps, LANES)
        chosen = jnp.concatenate(
            [wide_ref[part, pl.ds(0, taps, stride=2**level), :] for part in range(2)], axis=1
        )
        if rows > taps:
            chosen = jnp.concatenate([chosen, jnp.zeros((rows - taps, 2 * LANES), f32)], axis=0)
        taps_ref[at : at + rows, :] = chosen.astype(bf16)
        at, taps, level = at + rows, taps // 2, level + 1


def find_basis(mine, other, tap_rows, scale_down):
    first, first_spectrum = first_piece(mine[0], other[0], scale_down)
    half = mine[0].shape[0]
    length, rank = 2 * half, 2 * LANES
    return pl.pallas_call(
        functools.partial(basis_body, scale_down),
        out_shape=(
            jax.ShapeDtypeStruct((length, rank), bf16),
            jax.ShapeDtypeStruct((half, rank), bf16),
            jax.ShapeDtypeStruct((tap_rows, rank), bf16),
            jax.ShapeDtypeStruct((1, rank), f32),
        ),
        scratch_shapes=[pltpu.VMEM((length, LANES), f32), pltpu.VMEM((2, length, LANES), f32)],
        compiler_params=params(8),
        name="basis_second",
    )(first, first_spectrum, mine[1], other[1])


def level_sizes(levels, tap_count):
    return [max(1, (tap_count >> r) // LANES) for r in range(levels)]


def level_starts(total, levels):
    starts = [0]
    for r in range(levels):
        starts.append(starts[-1] + (total >> r))
    return starts


def levels_body(levels, detectors, history_ref, strain_ref, flipped_ref, level_ref):
    lead = history_ref.shape[1] // LANES
    each = lead + strain_ref.shape[1] // LANES
    total = detectors * each
    starts = level_starts(total, levels)
    source = iota((2 * LANES, 2 * LANES), 0)
    target = iota((2 * LANES, 2 * LANES), 1)
    even_odd = (source == 2 * (target % LANES) + target // LANES).astype(f32).astype(bf16)
    reverse = (
        iota((LANES, LANES), 0) + iota((LANES, LANES), 1) == LANES - 1
    ).astype(f32).astype(bf16)
    for d in range(detectors):
        for q in range(each):
            from_ref, at = (history_ref, q) if q < lead else (strain_ref, q - lead)
            level_ref[d * each + q : d * each + q + 1, :] = from_ref[
                d : d + 1, at * LANES : (at + 1) * LANES
            ]
    for r in range(levels):
        rows = total >> r
        at = starts[r]
        if r > 0:
            before = starts[r - 1]
            joined = jnp.concatenate(
                [
                    level_ref[pl.ds(before, rows, stride=2), :],
                    level_ref[pl.ds(before + 1, rows, stride=2), :],
                ],
                axis=1,
            )
            high, middle, low = split3(joined)
            both = (dot(high, even_odd) + dot(middle, even_odd)) + dot(low, even_odd)
            level_ref[at : at + rows, :] = (both[:, :LANES] + both[:, LANES:]) * inv_root_two
        rounded = level_ref[at : at + rows, :].astype(bf16)
        flipped_ref[at : at + rows, :] = dot(rounded, reverse)


def flipped_levels(history, strain, levels):
    detectors = strain.shape[0]
    total = detectors * (history.shape[1] + strain.shape[1]) // LANES
    held = -(-level_starts(total, levels)[-1] // SUBLANES) * SUBLANES
    return pl.pallas_call(
        functools.partial(levels_body, levels, detectors),
        out_shape=jax.ShapeDtypeStruct((held, LANES), f32),
        scratch_shapes=[pltpu.VMEM((held, LANES), f32)],
        compiler_params=params(6),
        name="strain_levels",
    )(history, strain)


def tiles_body(wanted, total, levels, blocks, detectors, chunks, flipped_ref, tiles_ref):
    step = pl.program_id(0)
    starts = level_starts(total, levels)
    detector = step // chunks
    chunk = step % chunks
    lower = iota((LANES, LANES), 1) <= iota((LANES, LANES), 0)
    at = 0
    for r in wanted:
        rows = (total >> r) // detectors
        history = (1 << (levels - 1)) >> r
        count = (rows - history) // chunks
        first = starts[r] + detector * rows + history + chunk * count - (blocks[r] - 1)

        def turned(row):
            line = jnp.broadcast_to(flipped_ref[pl.ds(row, 1), :], (LANES, LANES))
            return pltpu.roll(line, 1, 1, stride=1, stride_axis=0)

        before = turned(first - 1)
        for i in range(count + blocks[r] - 1):
            now = turned(first + i)
            tiles_ref[0, at] = jnp.where(lower, now, before).astype(bf16)
            before = now
            at += 1


def make_tiles(flipped, total, wanted, levels, blocks, detectors, chunks):
    count = 0
    for r in wanted:
        rows = (total >> r) // detectors
        lead = (1 << (levels - 1)) >> r
        count += (rows - lead) // chunks + blocks[r] - 1
    steps = detectors * chunks
    return pl.pallas_call(
        functools.partial(tiles_body, wanted, total, levels, blocks, detectors, chunks),
        grid=(steps,),
        out_shape=jax.ShapeDtypeStruct((steps, count, LANES, LANES), bf16),
        in_specs=[pl.BlockSpec(flipped.shape, lambda i: (0, 0))],
        out_specs=pl.BlockSpec((1, count, LANES, LANES), lambda i: (i, 0, 0, 0)),
        compiler_params=params(6),
        cost_estimate=pl.CostEstimate(
            flops=steps * count * LANES * LANES * 64,
            bytes_accessed=steps * count * LANES * LANES * 2, transcendentals=0,
        ),
        name="toeplitz_tiles",
    )(flipped)


def filter_body(blocks, chunks, unroll, tiles_ref, taps_ref, *refs):
    count = len(blocks)
    out_refs, held_refs = refs[:count], refs[count : 2 * count]
    here_ref, out_sem = tiles_ref, refs[2 * count]
    steps = tiles_ref.shape[0]

    def give(step, r):
        rows = out_refs[r].shape[2] // chunks
        spot = (step // chunks, pl.ds(step % chunks * rows, rows))
        return pltpu.make_async_copy(
            held_refs[r].at[spot], out_refs[r].at[(0, *spot)], out_sem.at[step, r]
        )

    def work(step):
        at, tap_at = 0, 0
        for r in range(count):
            rows = out_refs[r].shape[2] // chunks
            b = blocks[r]
            taps = taps_ref[tap_at : tap_at + b * LANES, :]
            group = min(rows, 512)
            for i in range(0, rows, group):
                first = at + b - 1 + i // LANES
                columns = [
                    here_ref[step, first - k : first - k + group // LANES].reshape(group, LANES)
                    for k in range(b)
                ]
                joined = jnp.concatenate(columns, axis=1) if b > 1 else columns[0]
                place = pl.ds(step % chunks * rows + i, group)
                held_refs[r][step // chunks, place, :] = dot(joined, taps).astype(bf16)
            give(step, r).start()
            at += rows // LANES + b - 1
            tap_at += b * LANES

    if unroll:
        for step in range(steps):
            work(step)
    else:
        pl.loop(0, steps)(work)
    for step in range(steps):
        for r in range(count):
            give(step, r).wait()


def filter_levels(tiles, taps, lengths, blocks, detectors, chunks, unroll=True):
    rank = taps.shape[1]
    steps = tiles.shape[0]
    anywhere = pl.BlockSpec(memory_space=pl.ANY)
    return pl.pallas_call(
        functools.partial(filter_body, blocks, chunks, unroll),
        out_shape=[jax.ShapeDtypeStruct((1, detectors, n, rank), bf16) for n in lengths],
        in_specs=[pl.BlockSpec(memory_space=pltpu.VMEM)] * 2,
        out_specs=[anywhere] * len(lengths),
        scratch_shapes=[pltpu.VMEM((detectors, n, rank), bf16) for n in lengths]
        + [pltpu.SemaphoreType.DMA((steps, len(lengths)))],
        compiler_params=params(18),
        cost_estimate=pl.CostEstimate(
            flops=2 * sum(n * b for n, b in zip(lengths, blocks)) * LANES * rank * detectors,
            bytes_accessed=2 * detectors * sum(lengths) * rank + 2 * math.prod(tiles.shape),
            transcendentals=0,
        ),
        name="filter_levels",
    )(tiles, taps)


def mixing_body(bins, grp, owner_ref, white_ref, own_ref, mine_ref, other_ref, out_ref, bases_ref):
    rows, width = white_ref.shape
    rank = own_ref.shape[1]
    half = width // 2
    core, here = lax.axis_index("grp") % 2, lax.axis_index("bin")
    bases_ref[0] = own_ref[...]
    bases_ref[1 + core] = mine_ref[:width]
    bases_ref[2 - core] = other_ref[:width]
    bases_ref[3, pl.ds(pl.multiple_of(core * half, half), half), :] = mine_ref[width:]
    bases_ref[3, pl.ds(pl.multiple_of((1 - core) * half, half), half), :] = other_ref[width:]
    mask = spread((owner_ref[...] // grp) ^ here, rows, bins, rank)
    white = white_ref[...]
    total = None
    for m in range(bins):
        chosen = mask[:, m * rank : (m + 1) * rank] > 0.5
        term = jnp.where(chosen, dot(white, bases_ref[m]), f32(0.0))
        total = term if total is None else total + term
    out_ref[...] = total.astype(bf16)


def mix(owner, white, own, mine, other, bins, grp):
    rows, width = white.shape
    rank = own.shape[1]
    return pl.pallas_call(
        functools.partial(mixing_body, bins, grp),
        out_shape=jax.ShapeDtypeStruct((rows, rank), bf16),
        scratch_shapes=[pltpu.VMEM((bins, width, rank), bf16)],
        compiler_params=params(14),
        name="mixing",
    )(owner, white, own, mine, other)


def local(templates, owner_device, rate_code, rate_gains, sketch, strain):
    rows, width = templates.shape
    grp = lax.axis_size("grp")
    bins = lax.axis_size("bin")
    levels = rate_gains.shape[0]
    detectors, samples = strain.shape
    owner = owner_device.reshape(1, rows)

    blocks = level_sizes(levels, width)
    chunks = 4
    reach = LANES << (levels - 1)
    total = detectors * (reach + samples) // LANES
    white, keep, send = front(
        owner, rate_code.reshape(1, rows), rate_gains, templates, sketch, bins, grp
    )

    def before(x, done):
        x, here = lax.optimization_barrier((x, strain))
        history = lax.ppermute(here[:, -reach:], "grp", [(i, i + 1) for i in range(grp - 1)])
        return x, (history,)

    def fine(x, done):
        x, history = lax.optimization_barrier((x, *done))
        flipped = flipped_levels(history, strain, levels)
        return x, (flipped, tiles_of(flipped, (0,)))

    def coarse(x, done):
        x, flipped, tiles = lax.optimization_barrier((x, *done))
        return x, (tiles, tiles_of(flipped, tuple(range(1, levels))))

    def tiles_of(flipped, wanted):
        return make_tiles(flipped, total, wanted, levels, blocks, detectors, chunks)

    mine, other, (tiles_fine, tiles_coarse) = reduce_products(
        keep, send, bins, grp, (before, fine, coarse)
    )
    own, part, taps, spectrum = find_basis(
        mine, other, sum(blocks[1:]) * LANES, rows * grp * math.sqrt(width)
    )
    near = flip_bin(own, (1, 2), bins, grp)
    far = flip_bin(part, (3, 3), bins, grp)
    lengths = [samples >> r for r in range(levels)]
    (finest,) = filter_levels(tiles_fine, own, lengths[:1], blocks[:1], detectors, chunks)
    near, far, finest = lax.optimization_barrier((near, far, finest))
    theirs = jnp.concatenate([near, far], axis=0)
    theirs_other = flip_core(theirs, grp)
    taps, theirs = lax.optimization_barrier((taps, theirs))
    filtered = filter_levels(tiles_coarse, taps, lengths[1:], blocks[1:], detectors, chunks)
    mixing = mix(owner, white, own, theirs, theirs_other, bins, grp)
    return (mixing, spectrum, finest, *filtered)


def solution(mesh):
    return jax.shard_map(
        local,
        mesh=mesh,
        in_specs=(
            P(("bin", "grp"), None),
            P(("bin", "grp"), None),
            P(("bin", "grp")),
            P(),
            P(),
            P(None, "grp"),
        ),
        out_specs=(
            P(("bin", "grp"), None),
            P("bin", None),
            P("bin", None, "grp", None),
            P("bin", None, "grp", None),
            P("bin", None, "grp", None),
            P("bin", None, "grp", None),
            P("bin", None, "grp", None),
        ),
        check_vma=False,
    )
```

```python
import functools
import math

import jax
import jax.numpy as jnp
from jax import lax
from jax.experimental import pallas as pl
from jax.experimental.pallas import tpu as pltpu
from jax.sharding import PartitionSpec as P

highest = lax.Precision.HIGHEST
inv_root_two = 0.7071067811865476
f32 = jnp.float32
bf16 = jnp.bfloat16
LANES = 128
SUBLANES = 8
MIB = 1024 * 1024


def iota(shape, axis):
    return lax.broadcasted_iota(jnp.int32, shape, axis)


def split3(x):
    high = x.astype(bf16)
    rest = x - high.astype(f32)
    middle = rest.astype(bf16)
    low = (rest - middle.astype(f32)).astype(bf16)
    return high, middle, low


def split2(x):
    high = x.astype(bf16)
    return high, (x - high.astype(f32)).astype(bf16)


def dot(a, b, precision=None):
    return jnp.dot(a, b, preferred_element_type=f32, precision=precision)


def dot_t(a, b, precision=None):
    return lax.dot_general(
        a, b, (((0,), (0,)), ((), ())), preferred_element_type=f32, precision=precision
    )


def params(mib):
    return pltpu.CompilerParams(vmem_limit_bytes=mib * MIB)


def spread(group, rows, groups, width):
    member = (iota((8, rows), 0) == group).astype(f32).astype(bf16)
    column = (iota((8, groups * width), 0) == iota((8, groups * width), 1) // width).astype(f32)
    return dot_t(member, column.astype(bf16))


def front_body(bins, grp, owner_ref, code_ref, gains_hbm, templates_hbm, sketch_hbm, white_hbm, keep_hbm,
               send_hbm, gains_ref, templates_ref, sketch_ref, white_ref, sketched_ref, keep_ref, send_ref,
               sem, out_sem):
    rows, width = templates_ref.shape
    rates = gains_ref.shape[0]
    pieces = 4
    piece = rows // pieces
    copies = [
        pltpu.make_async_copy(gains_hbm, gains_ref, sem.at[0]),
        pltpu.make_async_copy(sketch_hbm, sketch_ref, sem.at[1]),
    ]
    for i in range(pieces):
        at = pl.ds(i * piece, piece)
        copies.append(
            pltpu.make_async_copy(templates_hbm.at[at], templates_ref.at[at], sem.at[2 + i])
        )
    for copy in copies:
        copy.start()
    given = [
        pltpu.make_async_copy(white_ref, white_hbm, out_sem.at[0]),
        pltpu.make_async_copy(send_ref, send_hbm, out_sem.at[1]),
        pltpu.make_async_copy(keep_ref, keep_hbm, out_sem.at[2]),
    ]
    member = (iota((8, rows), 0) == code_ref[...]).astype(f32)
    member = jnp.concatenate([member, member, member], axis=0).astype(bf16)
    mask = spread(owner_ref[...] // grp, rows, bins, LANES).astype(bf16)
    copies[0].wait()
    gains = jnp.concatenate([gains_ref[...], jnp.zeros((8 - rates, width), f32)], axis=0)
    parts = jnp.concatenate([part.astype(f32) for part in split3(gains)], axis=0).astype(bf16)
    copies[1].wait()
    sketch_parts = split2(sketch_ref[...])
    for i in range(pieces):
        at = slice(i * piece, (i + 1) * piece)
        factor = dot_t(member[:, at], parts)
        copies[2 + i].wait()
        white = (templates_ref[at, :].astype(f32) * factor).astype(bf16)
        white_ref[at, :] = white
        sketched = None
        for part in sketch_parts:
            term = dot(white, part)
            sketched = term if sketched is None else sketched + term
        sketched_ref[at, :] = sketched
    given[0].start()
    core = lax.axis_index("grp") % 2
    sketched_parts = split2(sketched_ref[...])
    products(bins, 1 - core, mask, white_ref, sketched_parts, send_ref)
    given[1].start()
    products(bins, core, mask, white_ref, sketched_parts, keep_ref)
    given[2].start()
    for copy in given:
        copy.wait()


def products(bins, which, mask, white_ref, sketched_parts, out_ref):
    rows, width = white_ref.shape
    half = width // 2
    chosen = white_ref[:, pl.ds(pl.multiple_of(which * half, half), half)]
    masked = jnp.concatenate(
        [
            chosen * jnp.concatenate([mask[:, b * LANES : (b + 1) * LANES]] * (half // LANES), axis=1)
            for b in range(bins)
        ],
        axis=1,
    )
    total = None
    for part in sketched_parts:
        term = dot_t(masked, part)
        total = term if total is None else total + term
    for b in range(bins):
        high, low = b // 2, b % 2
        one, two = jnp.where(which == 0, low, high), jnp.where(which == 0, high, low)
        for i in range(out_ref.shape[0]):
            out_ref[i, one, two] = total[b * half : (b + 1) * half, i * LANES : (i + 1) * LANES]


def halves(bins, width, rank):
    return (rank // LANES, 2, bins // 2, width // 2, LANES)


def front(owner, code, gains, templates, sketch, bins, grp):
    rows, width = templates.shape
    rank = sketch.shape[1]
    vmem, anywhere = pl.BlockSpec(memory_space=pltpu.VMEM), pl.BlockSpec(memory_space=pl.ANY)
    sent = halves(bins, width, rank)
    return pl.pallas_call(
        functools.partial(front_body, bins, grp),
        out_shape=(
            jax.ShapeDtypeStruct((rows, width), bf16),
            jax.ShapeDtypeStruct(sent, f32),
            jax.ShapeDtypeStruct(sent, f32),
        ),
        in_specs=[vmem, vmem, anywhere, anywhere, anywhere],
        out_specs=(anywhere, anywhere, anywhere),
        scratch_shapes=[
            pltpu.VMEM(gains.shape, f32),
            pltpu.VMEM(templates.shape, bf16),
            pltpu.VMEM(sketch.shape, f32),
            pltpu.VMEM((rows, width), bf16),
            pltpu.VMEM((rows, rank), f32),
            pltpu.VMEM(sent, f32),
            pltpu.VMEM(sent, f32),
            pltpu.SemaphoreType.DMA((6,)),
            pltpu.SemaphoreType.DMA((3,)),
        ],
        compiler_params=params(60),
        name="whiten_products",
    )(owner, code, gains, templates, sketch)


def pick(x, index):
    return lax.dynamic_index_in_dim(x, index, 0, keepdims=False)


def flip_bin(x, bits, bins, grp):
    pairs = [
        (b * grp + g, (b ^ bits[g % 2]) * grp + g) for b in range(bins) for g in range(grp)
    ]
    return lax.ppermute(x, ("bin", "grp"), pairs)


def flip_core(x, grp):
    return lax.ppermute(x, "grp", [(i, i ^ 1) for i in range(grp)])


def flip_chip(x, bits, grp):
    return lax.ppermute(x, "grp", [(i, i ^ (2 * bits[i % 2])) for i in range(grp)])


def reduce_products(keep, send, bins, grp, beside):
    keep, done = beside[0](keep, ())
    came = flip_core(send, grp)
    came, done = beside[1](came, done)
    here = lax.axis_index("bin")
    core = lax.axis_index("grp") % 2
    high, low = here >> 1, here & 1
    one, two = jnp.where(core == 0, low, high), jnp.where(core == 0, high, low)
    pieces = range(keep.shape[0])

    def stage(held, leaving, move):
        arrived = [move(x) for x in leaving]
        return [x + y for x, y in zip(held, arrived)]

    def side(which):
        return jnp.stack([pick(keep[i], which) + pick(came[i], which) for i in pieces])

    arrived = flip_bin(side(1 - one), (1, 2), bins, grp)
    arrived, *done = lax.optimization_barrier((arrived, *done))
    total = [pick(keep[i], one) + pick(came[i], one) + arrived[i] for i in pieces]
    total[-1], done = beside[2](total[-1], done)
    mine = stage(
        [pick(x, two) for x in total],
        [pick(x, 1 - two) for x in total],
        lambda x: flip_bin(x, (2, 1), bins, grp),
    )
    bits = [1 << i for i in range((grp // 2).bit_length() - 1)]
    mine[-1], *done = lax.optimization_barrier((mine[-1], *done))
    mine[-1], done = beside[3](mine[-1], done)
    for step, bit in enumerate(bits):
        mine = stage(mine, mine, lambda x: flip_chip(x, (bit, bits[-1 - step]), grp))
        if step == 0:
            mine[-1], *done = lax.optimization_barrier((mine[-1], *done))
    return mine, [flip_core(x, grp) for x in mine], done


def eliminate(state):
    finished = []
    size = state.shape[0]
    head = iota((SUBLANES, size), 0)

    def spread_column(rows, column):
        return jnp.broadcast_to(rows[:, column : column + 1], rows.shape)

    tops = [spread_column(state[:SUBLANES], k) for k in range(SUBLANES)]
    for start in range(0, size, SUBLANES):
        after = start + SUBLANES
        eye = iota((SUBLANES, size), 1) == head + start
        top, rest = state[:SUBLANES], state[SUBLANES:]
        more = rest.shape[0] > 0
        rests = [spread_column(rest, start + k) for k in range(SUBLANES)] if more else []
        nexts = [spread_column(rest[:SUBLANES], after + k) for k in range(SUBLANES)] if more else []
        top = jnp.where(eye, f32(1.0), jnp.where(in_lanes(top, start, after), f32(0.0), top))
        if more:
            rest = jnp.where(in_lanes(rest, start, after), f32(0.0), rest)
        pivots = jnp.zeros((SUBLANES, size), f32)
        for k in range(SUBLANES):
            pivot = tops[k][k : k + 1]
            inverse = 1.0 / pivot
            below = jnp.where(head > k, tops[k], f32(0.0))
            factor = rests[k] * inverse if more else None
            for j in range(k + 1, SUBLANES):
                across = tops[j][k : k + 1]
                tops[j] = tops[j] - (below * across) * inverse
                if more:
                    rests[j] = rests[j] - factor * across
            if more:
                for j in range(SUBLANES):
                    nexts[j] = nexts[j] - factor[:SUBLANES] * rests[k][j : j + 1]
            across = top[k : k + 1]
            top = top - (below * across) * inverse
            if more:
                rest = rest - factor * across
            pivots = jnp.where(head == k, pivot, pivots)
        finished.append(top * lax.rsqrt(pivots))
        state, tops = rest, nexts
    inverse = jnp.concatenate(finished, axis=0)
    return jnp.where(iota((size, size), 0) >= iota((size, size), 1), inverse, f32(0.0))


def in_lanes(x, first, end):
    lane = iota(x.shape, 1)
    return (lane >= first) & (lane < end)


def joined_rows(mine_ref, other_ref, product_ref):
    half = mine_ref.shape[0]
    core = lax.axis_index("grp") % 2
    product_ref[pl.ds(pl.multiple_of(core * half, half), half), :] = mine_ref[...]
    product_ref[pl.ds(pl.multiple_of((1 - core) * half, half), half), :] = other_ref[...]
    return product_ref[...]


def basis_piece(scale_down, product, before):
    inner = dot_t(product, product, highest)
    rest = product
    for basis in before:
        across = dot_t(basis, product, highest)
        inner = inner - dot_t(across, across, highest)
        rest = rest - dot(basis, across, highest)
    inverse = eliminate(inner)
    basis = lax.dot_general(
        rest, inverse, (((1,), (1,)), ((), ())), preferred_element_type=f32, precision=highest
    )
    eye = iota(inverse.shape, 0) == iota(inverse.shape, 1)
    diagonal = jnp.sum(jnp.where(eye, inverse, f32(0.0)), axis=0, keepdims=True)
    return basis, (1.0 / diagonal) / scale_down


def piece_body(scale_down, mine_ref, other_ref, basis_ref, spectrum_ref, product_ref):
    product = joined_rows(mine_ref, other_ref, product_ref)
    basis_ref[...], spectrum_ref[...] = basis_piece(scale_down, product, [])


def first_piece(mine, other, scale_down):
    half, columns = mine.shape
    return pl.pallas_call(
        functools.partial(piece_body, scale_down),
        out_shape=(
            jax.ShapeDtypeStruct((2 * half, columns), f32),
            jax.ShapeDtypeStruct((1, columns), f32),
        ),
        scratch_shapes=[pltpu.VMEM((2 * half, columns), f32)],
        compiler_params=params(8),
        name="basis_first",
    )(mine, other)


def basis_body(scale_down, first_ref, first_spectrum_ref, mine_ref, other_ref, own_ref, part_ref, taps_ref,
               spectrum_ref, product_ref, wide_ref):
    half = mine_ref.shape[0]
    core = lax.axis_index("grp") % 2
    product = joined_rows(mine_ref, other_ref, product_ref)
    first = first_ref[...]
    wide_ref[0] = first
    wide_ref[1], spectrum_ref[:, LANES:] = basis_piece(scale_down, product, [first])
    spectrum_ref[:, :LANES] = first_spectrum_ref[...]
    own_ref[...] = jnp.concatenate([wide_ref[0], wide_ref[1]], axis=1).astype(bf16)
    part_ref[...] = own_ref[pl.ds(pl.multiple_of(core * half, half), half), :]
    at = 0
    taps, level = half, 1
    while at < taps_ref.shape[0]:
        rows = max(taps, LANES)
        chosen = jnp.concatenate(
            [wide_ref[part, pl.ds(0, taps, stride=2**level), :] for part in range(2)], axis=1
        )
        if rows > taps:
            chosen = jnp.concatenate([chosen, jnp.zeros((rows - taps, 2 * LANES), f32)], axis=0)
        taps_ref[at : at + rows, :] = chosen.astype(bf16)
        at, taps, level = at + rows, taps // 2, level + 1


def find_basis(mine, other, tap_rows, scale_down):
    first, first_spectrum = first_piece(mine[0], other[0], scale_down)
    half = mine[0].shape[0]
    length, rank = 2 * half, 2 * LANES
    return pl.pallas_call(
        functools.partial(basis_body, scale_down),
        out_shape=(
            jax.ShapeDtypeStruct((length, rank), bf16),
            jax.ShapeDtypeStruct((half, rank), bf16),
            jax.ShapeDtypeStruct((tap_rows, rank), bf16),
            jax.ShapeDtypeStruct((1, rank), f32),
        ),
        scratch_shapes=[pltpu.VMEM((length, LANES), f32), pltpu.VMEM((2, length, LANES), f32)],
        compiler_params=params(8),
        name="basis_second",
    )(first, first_spectrum, mine[1], other[1])


def level_sizes(levels, tap_count):
    return [max(1, (tap_count >> r) // LANES) for r in range(levels)]


def level_starts(total, levels):
    starts = [0]
    for r in range(levels):
        starts.append(starts[-1] + (total >> r))
    return starts


def levels_body(levels, detectors, history_ref, strain_ref, flipped_ref, level_ref):
    lead = history_ref.shape[1] // LANES
    each = lead + strain_ref.shape[1] // LANES
    total = detectors * each
    starts = level_starts(total, levels)
    source = iota((2 * LANES, 2 * LANES), 0)
    target = iota((2 * LANES, 2 * LANES), 1)
    even_odd = (source == 2 * (target % LANES) + target // LANES).astype(f32).astype(bf16)
    reverse = (
        iota((LANES, LANES), 0) + iota((LANES, LANES), 1) == LANES - 1
    ).astype(f32).astype(bf16)
    for d in range(detectors):
        for q in range(each):
            from_ref, at = (history_ref, q) if q < lead else (strain_ref, q - lead)
            level_ref[d * each + q : d * each + q + 1, :] = from_ref[
                d : d + 1, at * LANES : (at + 1) * LANES
            ]
    for r in range(levels):
        rows = total >> r
        at = starts[r]
        if r > 0:
            before = starts[r - 1]
            joined = jnp.concatenate(
                [
                    level_ref[pl.ds(before, rows, stride=2), :],
                    level_ref[pl.ds(before + 1, rows, stride=2), :],
                ],
                axis=1,
            )
            high, middle, low = split3(joined)
            both = (dot(high, even_odd) + dot(middle, even_odd)) + dot(low, even_odd)
            level_ref[at : at + rows, :] = (both[:, :LANES] + both[:, LANES:]) * inv_root_two
        rounded = level_ref[at : at + rows, :].astype(bf16)
        flipped_ref[at : at + rows, :] = dot(rounded, reverse)


def flipped_levels(history, strain, levels):
    detectors = strain.shape[0]
    total = detectors * (history.shape[1] + strain.shape[1]) // LANES
    held = -(-level_starts(total, levels)[-1] // SUBLANES) * SUBLANES
    return pl.pallas_call(
        functools.partial(levels_body, levels, detectors),
        out_shape=jax.ShapeDtypeStruct((held, LANES), f32),
        scratch_shapes=[pltpu.VMEM((held, LANES), f32)],
        compiler_params=params(6),
        name="strain_levels",
    )(history, strain)


def tiles_body(wanted, total, levels, blocks, detectors, chunks, flipped_ref, tiles_ref):
    step = pl.program_id(0)
    starts = level_starts(total, levels)
    detector = step // chunks
    chunk = step % chunks
    lower = iota((LANES, LANES), 1) <= iota((LANES, LANES), 0)
    at = 0
    for r in wanted:
        rows = (total >> r) // detectors
        history = (1 << (levels - 1)) >> r
        count = (rows - history) // chunks
        first = starts[r] + detector * rows + history + chunk * count - (blocks[r] - 1)

        def turned(row):
            line = jnp.broadcast_to(flipped_ref[pl.ds(row, 1), :], (LANES, LANES))
            return pltpu.roll(line, 1, 1, stride=1, stride_axis=0)

        before = turned(first - 1)
        for i in range(count + blocks[r] - 1):
            now = turned(first + i)
            tiles_ref[0, at] = jnp.where(lower, now, before).astype(bf16)
            before = now
            at += 1


def make_tiles(flipped, total, wanted, levels, blocks, detectors, chunks):
    count = 0
    for r in wanted:
        rows = (total >> r) // detectors
        lead = (1 << (levels - 1)) >> r
        count += (rows - lead) // chunks + blocks[r] - 1
    steps = detectors * chunks
    return pl.pallas_call(
        functools.partial(tiles_body, wanted, total, levels, blocks, detectors, chunks),
        grid=(steps,),
        out_shape=jax.ShapeDtypeStruct((steps, count, LANES, LANES), bf16),
        in_specs=[pl.BlockSpec(flipped.shape, lambda i: (0, 0))],
        out_specs=pl.BlockSpec((1, count, LANES, LANES), lambda i: (i, 0, 0, 0)),
        compiler_params=params(6),
        cost_estimate=pl.CostEstimate(
            flops=steps * count * LANES * LANES * 64,
            bytes_accessed=steps * count * LANES * LANES * 2, transcendentals=0,
        ),
        name="toeplitz_tiles",
    )(flipped)


def filter_body(blocks, chunks, tiles_ref, taps_ref, *refs):
    count = len(blocks)
    out_refs, held_refs = refs[:count], refs[count : 2 * count]
    here_ref, out_sem = tiles_ref, refs[2 * count]
    steps = tiles_ref.shape[0]

    def give(step, r):
        rows = out_refs[r].shape[2] // chunks
        spot = (step // chunks, pl.ds(step % chunks * rows, rows))
        return pltpu.make_async_copy(
            held_refs[r].at[spot], out_refs[r].at[(0, *spot)], out_sem.at[step, r]
        )

    def work(step):
        at, tap_at = 0, 0
        for r in range(count):
            rows = out_refs[r].shape[2] // chunks
            b = blocks[r]
            taps = taps_ref[tap_at : tap_at + b * LANES, :]
            group = min(rows, 512)
            for i in range(0, rows, group):
                first = at + b - 1 + i // LANES
                columns = [
                    here_ref[step, first - k : first - k + group // LANES].reshape(group, LANES)
                    for k in range(b)
                ]
                joined = jnp.concatenate(columns, axis=1) if b > 1 else columns[0]
                place = pl.ds(step % chunks * rows + i, group)
                held_refs[r][step // chunks, place, :] = dot(joined, taps).astype(bf16)
            give(step, r).start()
            at += rows // LANES + b - 1
            tap_at += b * LANES

    for step in range(steps):
        work(step)
    for step in range(steps):
        for r in range(count):
            give(step, r).wait()


def filter_levels(tiles, taps, lengths, blocks, detectors, chunks):
    rank = taps.shape[1]
    steps = tiles.shape[0]
    anywhere = pl.BlockSpec(memory_space=pl.ANY)
    return pl.pallas_call(
        functools.partial(filter_body, blocks, chunks),
        out_shape=[jax.ShapeDtypeStruct((1, detectors, n, rank), bf16) for n in lengths],
        in_specs=[pl.BlockSpec(memory_space=pltpu.VMEM)] * 2,
        out_specs=[anywhere] * len(lengths),
        scratch_shapes=[pltpu.VMEM((detectors, n, rank), bf16) for n in lengths]
        + [pltpu.SemaphoreType.DMA((steps, len(lengths)))],
        compiler_params=params(18),
        cost_estimate=pl.CostEstimate(
            flops=2 * sum(n * b for n, b in zip(lengths, blocks)) * LANES * rank * detectors,
            bytes_accessed=2 * detectors * sum(lengths) * rank + 2 * math.prod(tiles.shape),
            transcendentals=0,
        ),
        name="filter_levels",
    )(tiles, taps)


def mixing_body(bins, grp, owner_ref, white_ref, own_ref, mine_ref, other_ref, out_hbm, bases_ref, out_ref,
                sem):
    rows, width = white_ref.shape
    half = width // 2
    core, here = lax.axis_index("grp") % 2, lax.axis_index("bin")

    def place(row, count):
        return pl.ds(pl.multiple_of(row, count), count)

    bases_ref[:width] = own_ref[...]
    bases_ref[place((1 + core) * width, width), :] = mine_ref[:width]
    bases_ref[place((2 - core) * width, width), :] = other_ref[:width]
    bases_ref[place(3 * width + core * half, half), :] = mine_ref[width:]
    bases_ref[place(3 * width + (1 - core) * half, half), :] = other_ref[width:]
    mask = spread((owner_ref[...] // grp) ^ here, rows, bins, LANES).astype(bf16)
    pieces = 4
    piece = rows // pieces
    given = []
    for i in range(pieces):
        at = slice(i * piece, (i + 1) * piece)
        white = white_ref[at, :]
        masked = jnp.concatenate(
            [
                white * jnp.concatenate([mask[at, m * LANES : (m + 1) * LANES]] * (width // LANES), axis=1)
                for m in range(bins)
            ],
            axis=1,
        )
        out_ref[at, :] = dot(masked, bases_ref[...]).astype(bf16)
        rows_at = pl.ds(i * piece, piece)
        given.append(pltpu.make_async_copy(out_ref.at[rows_at], out_hbm.at[rows_at], sem.at[i]))
        given[-1].start()
    for copy in given:
        copy.wait()


def mix(owner, white, own, mine, other, bins, grp):
    rows, width = white.shape
    rank = own.shape[1]
    return pl.pallas_call(
        functools.partial(mixing_body, bins, grp),
        out_shape=jax.ShapeDtypeStruct((rows, rank), bf16),
        in_specs=[pl.BlockSpec(memory_space=pltpu.VMEM)] * 5,
        out_specs=pl.BlockSpec(memory_space=pl.ANY),
        scratch_shapes=[
            pltpu.VMEM((bins * width, rank), bf16),
            pltpu.VMEM((rows, rank), bf16),
            pltpu.SemaphoreType.DMA((4,)),
        ],
        compiler_params=params(14),
        name="mixing",
    )(owner, white, own, mine, other)


def local(templates, owner_device, rate_code, rate_gains, sketch, strain):
    rows, width = templates.shape
    grp = lax.axis_size("grp")
    bins = lax.axis_size("bin")
    levels = rate_gains.shape[0]
    detectors, samples = strain.shape
    owner = owner_device.reshape(1, rows)

    blocks = level_sizes(levels, width)
    chunks = 4
    reach = LANES << (levels - 1)
    total = detectors * (reach + samples) // LANES
    white, keep, send = front(
        owner, rate_code.reshape(1, rows), rate_gains, templates, sketch, bins, grp
    )

    def before(x, done):
        x, here = lax.optimization_barrier((x, strain))
        history = lax.ppermute(here[:, -reach:], "grp", [(i, i + 1) for i in range(grp - 1)])
        return x, (history,)

    def lines(x, done):
        return x, (flipped_levels(*done, strain, levels),)

    def tiles_of(wanted):
        def work(x, done):
            x, flipped, *rest = lax.optimization_barrier((x, *done))
            tiles = make_tiles(flipped, total, wanted, levels, blocks, detectors, chunks)
            return x, (flipped, *rest, tiles)

        return work

    mine, other, (_, tiles_coarse, tiles_fine) = reduce_products(
        keep, send, bins, grp, (before, lines, tiles_of(tuple(range(1, levels))), tiles_of((0,)))
    )
    own, part, taps, spectrum = find_basis(
        mine, other, sum(blocks[1:]) * LANES, rows * grp * math.sqrt(width)
    )
    near = flip_bin(own, (1, 2), bins, grp)
    far = flip_bin(part, (3, 3), bins, grp)
    lengths = [samples >> r for r in range(levels)]
    (finest,) = filter_levels(tiles_fine, own, lengths[:1], blocks[:1], detectors, chunks)
    near, far, finest = lax.optimization_barrier((near, far, finest))
    theirs = jnp.concatenate([near, far], axis=0)
    theirs_other = flip_core(theirs, grp)
    taps, theirs = lax.optimization_barrier((taps, theirs))
    filtered = filter_levels(tiles_coarse, taps, lengths[1:], blocks[1:], detectors, chunks)
    mixing = mix(owner, white, own, theirs, theirs_other, bins, grp)
    return (mixing, spectrum, finest, *filtered)


def solution(mesh):
    return jax.shard_map(
        local,
        mesh=mesh,
        in_specs=(
            P(("bin", "grp"), None),
            P(("bin", "grp"), None),
            P(("bin", "grp")),
            P(),
            P(),
            P(None, "grp"),
        ),
        out_specs=(
            P(("bin", "grp"), None),
            P("bin", None),
            P("bin", None, "grp", None),
            P("bin", None, "grp", None),
            P("bin", None, "grp", None),
            P("bin", None, "grp", None),
            P("bin", None, "grp", None),
        ),
        check_vma=False,
    )
```

```python
import functools
import math

import jax
import jax.numpy as jnp
from jax import lax
from jax.experimental import pallas as pl
from jax.experimental.pallas import tpu as pltpu
from jax.sharding import PartitionSpec as P

highest = lax.Precision.HIGHEST
inv_root_two = 0.7071067811865476
f32 = jnp.float32
bf16 = jnp.bfloat16
LANES = 128
SUBLANES = 8
MIB = 1024 * 1024


def iota(shape, axis):
    return lax.broadcasted_iota(jnp.int32, shape, axis)


def split3(x):
    high = x.astype(bf16)
    rest = x - high.astype(f32)
    middle = rest.astype(bf16)
    low = (rest - middle.astype(f32)).astype(bf16)
    return high, middle, low


def split2(x):
    high = x.astype(bf16)
    return high, (x - high.astype(f32)).astype(bf16)


def dot(a, b, precision=None):
    return jnp.dot(a, b, preferred_element_type=f32, precision=precision)


def dot_t(a, b, precision=None):
    return lax.dot_general(
        a, b, (((0,), (0,)), ((), ())), preferred_element_type=f32, precision=precision
    )


def params(mib):
    return pltpu.CompilerParams(vmem_limit_bytes=mib * MIB)


def spread(group, rows, groups, width):
    member = (iota((8, rows), 0) == group).astype(f32).astype(bf16)
    column = (iota((8, groups * width), 0) == iota((8, groups * width), 1) // width).astype(f32)
    return dot_t(member, column.astype(bf16))


def front_body(bins, grp, owner_ref, code_ref, gains_hbm, templates_hbm, sketch_hbm, white_hbm, keep_hbm,
               send_hbm, gains_ref, templates_ref, sketch_ref, white_ref, sketched_ref, keep_ref, send_ref,
               sem, out_sem):
    rows, width = templates_ref.shape
    rates = gains_ref.shape[0]
    pieces = 2
    piece = rows // pieces
    copies = [
        pltpu.make_async_copy(gains_hbm, gains_ref, sem.at[0]),
        pltpu.make_async_copy(sketch_hbm, sketch_ref, sem.at[1]),
    ]
    for i in range(pieces):
        at = pl.ds(i * piece, piece)
        copies.append(
            pltpu.make_async_copy(templates_hbm.at[at], templates_ref.at[at], sem.at[2 + i])
        )
    for copy in copies:
        copy.start()
    given = [
        pltpu.make_async_copy(white_ref, white_hbm, out_sem.at[0]),
        pltpu.make_async_copy(send_ref, send_hbm, out_sem.at[1]),
        pltpu.make_async_copy(keep_ref, keep_hbm, out_sem.at[2]),
    ]
    member = (iota((8, rows), 0) == code_ref[...]).astype(f32)
    member = jnp.concatenate([member, member, member], axis=0).astype(bf16)
    mask = spread(owner_ref[...] // grp, rows, bins, LANES).astype(bf16)
    copies[0].wait()
    gains = jnp.concatenate([gains_ref[...], jnp.zeros((8 - rates, width), f32)], axis=0)
    parts = jnp.concatenate([part.astype(f32) for part in split3(gains)], axis=0).astype(bf16)
    copies[1].wait()
    sketch_parts = split2(sketch_ref[...])
    for i in range(pieces):
        at = slice(i * piece, (i + 1) * piece)
        factor = dot_t(member[:, at], parts)
        copies[2 + i].wait()
        white = (templates_ref[at, :].astype(f32) * factor).astype(bf16)
        white_ref[at, :] = white
        sketched = None
        for part in sketch_parts:
            term = dot(white, part)
            sketched = term if sketched is None else sketched + term
        sketched_ref[at, :] = sketched
    given[0].start()
    core = lax.axis_index("grp") % 2
    sketched_parts = split2(sketched_ref[...])
    products(bins, 1 - core, mask, white_ref, sketched_parts, send_ref)
    given[1].start()
    products(bins, core, mask, white_ref, sketched_parts, keep_ref)
    given[2].start()
    for copy in given:
        copy.wait()


def products(bins, which, mask, white_ref, sketched_parts, out_ref):
    rows, width = white_ref.shape
    half = width // 2
    chosen = white_ref[:, pl.ds(pl.multiple_of(which * half, half), half)]
    masked = jnp.concatenate(
        [
            chosen * jnp.concatenate([mask[:, b * LANES : (b + 1) * LANES]] * (half // LANES), axis=1)
            for b in range(bins)
        ],
        axis=1,
    )
    total = None
    for part in sketched_parts:
        term = dot_t(masked, part)
        total = term if total is None else total + term
    for b in range(bins):
        high, low = b // 2, b % 2
        one, two = jnp.where(which == 0, low, high), jnp.where(which == 0, high, low)
        for i in range(out_ref.shape[0]):
            out_ref[i, one, two] = total[b * half : (b + 1) * half, i * LANES : (i + 1) * LANES]


def halves(bins, width, rank):
    return (rank // LANES, 2, bins // 2, width // 2, LANES)


def front(owner, code, gains, templates, sketch, bins, grp):
    rows, width = templates.shape
    rank = sketch.shape[1]
    vmem, anywhere = pl.BlockSpec(memory_space=pltpu.VMEM), pl.BlockSpec(memory_space=pl.ANY)
    sent = halves(bins, width, rank)
    return pl.pallas_call(
        functools.partial(front_body, bins, grp),
        out_shape=(
            jax.ShapeDtypeStruct((rows, width), bf16),
            jax.ShapeDtypeStruct(sent, f32),
            jax.ShapeDtypeStruct(sent, f32),
        ),
        in_specs=[vmem, vmem, anywhere, anywhere, anywhere],
        out_specs=(anywhere, anywhere, anywhere),
        scratch_shapes=[
            pltpu.VMEM(gains.shape, f32),
            pltpu.VMEM(templates.shape, bf16),
            pltpu.VMEM(sketch.shape, f32),
            pltpu.VMEM((rows, width), bf16),
            pltpu.VMEM((rows, rank), f32),
            pltpu.VMEM(sent, f32),
            pltpu.VMEM(sent, f32),
            pltpu.SemaphoreType.DMA((6,)),
            pltpu.SemaphoreType.DMA((3,)),
        ],
        compiler_params=params(60),
        name="whiten_products",
    )(owner, code, gains, templates, sketch)


def pick(x, index):
    return lax.dynamic_index_in_dim(x, index, 0, keepdims=False)


def flip_bin(x, bits, bins, grp):
    pairs = [
        (b * grp + g, (b ^ bits[g % 2]) * grp + g) for b in range(bins) for g in range(grp)
    ]
    return lax.ppermute(x, ("bin", "grp"), pairs)


def flip_core(x, grp):
    return lax.ppermute(x, "grp", [(i, i ^ 1) for i in range(grp)])


def flip_chip(x, bits, grp):
    return lax.ppermute(x, "grp", [(i, i ^ (2 * bits[i % 2])) for i in range(grp)])


def reduce_products(keep, send, bins, grp, beside):
    keep, done = beside[0](keep, ())
    came = flip_core(send, grp)
    came, done = beside[1](came, done)
    here = lax.axis_index("bin")
    core = lax.axis_index("grp") % 2
    high, low = here >> 1, here & 1
    one, two = jnp.where(core == 0, low, high), jnp.where(core == 0, high, low)
    pieces = range(keep.shape[0])

    def stage(held, leaving, move):
        arrived = [move(x) for x in leaving]
        return [x + y for x, y in zip(held, arrived)]

    def side(which):
        return jnp.stack([pick(keep[i], which) + pick(came[i], which) for i in pieces])

    arrived = flip_bin(side(1 - one), (1, 2), bins, grp)
    arrived, *done = lax.optimization_barrier((arrived, *done))
    total = [pick(keep[i], one) + pick(came[i], one) + arrived[i] for i in pieces]
    total[-1], done = beside[2](total[-1], done)
    mine = stage(
        [pick(x, two) for x in total],
        [pick(x, 1 - two) for x in total],
        lambda x: flip_bin(x, (2, 1), bins, grp),
    )
    bits = [1 << i for i in range((grp // 2).bit_length() - 1)]
    mine[-1], *done = lax.optimization_barrier((mine[-1], *done))
    for step, bit in enumerate(bits):
        if step == len(bits) - 1:
            mine[-1], done = beside[3](mine[-1], done)
        mine = stage(mine, mine, lambda x: flip_chip(x, (bit, bits[-1 - step]), grp))
    mine[-1], *done = lax.optimization_barrier((mine[-1], *done))
    return mine, [flip_core(x, grp) for x in mine], done


def eliminate(state):
    finished = []
    size = state.shape[0]
    head = iota((SUBLANES, size), 0)

    def spread_column(rows, column):
        return jnp.broadcast_to(rows[:, column : column + 1], rows.shape)

    tops = [spread_column(state[:SUBLANES], k) for k in range(SUBLANES)]
    for start in range(0, size, SUBLANES):
        after = start + SUBLANES
        eye = iota((SUBLANES, size), 1) == head + start
        top, rest = state[:SUBLANES], state[SUBLANES:]
        more = rest.shape[0] > 0
        rests = [spread_column(rest, start + k) for k in range(SUBLANES)] if more else []
        nexts = [spread_column(rest[:SUBLANES], after + k) for k in range(SUBLANES)] if more else []
        top = jnp.where(eye, f32(1.0), jnp.where(in_lanes(top, start, after), f32(0.0), top))
        if more:
            rest = jnp.where(in_lanes(rest, start, after), f32(0.0), rest)
        pivots = jnp.zeros((SUBLANES, size), f32)
        for k in range(SUBLANES):
            pivot = tops[k][k : k + 1]
            inverse = 1.0 / pivot
            below = jnp.where(head > k, tops[k], f32(0.0))
            factor = rests[k] * inverse if more else None
            for j in range(k + 1, SUBLANES):
                across = tops[j][k : k + 1]
                tops[j] = tops[j] - (below * across) * inverse
                if more:
                    rests[j] = rests[j] - factor * across
            if more:
                for j in range(SUBLANES):
                    nexts[j] = nexts[j] - factor[:SUBLANES] * rests[k][j : j + 1]
            across = top[k : k + 1]
            top = top - (below * across) * inverse
            if more:
                rest = rest - factor * across
            pivots = jnp.where(head == k, pivot, pivots)
        finished.append(top * lax.rsqrt(pivots))
        state, tops = rest, nexts
    inverse = jnp.concatenate(finished, axis=0)
    return jnp.where(iota((size, size), 0) >= iota((size, size), 1), inverse, f32(0.0))


def in_lanes(x, first, end):
    lane = iota(x.shape, 1)
    return (lane >= first) & (lane < end)


def joined_rows(mine_ref, other_ref, product_ref):
    half = mine_ref.shape[0]
    core = lax.axis_index("grp") % 2
    product_ref[pl.ds(pl.multiple_of(core * half, half), half), :] = mine_ref[...]
    product_ref[pl.ds(pl.multiple_of((1 - core) * half, half), half), :] = other_ref[...]
    return product_ref[...]


def basis_piece(scale_down, product, before):
    inner = dot_t(product, product, highest)
    rest = product
    for basis in before:
        across = dot_t(basis, product, highest)
        inner = inner - dot_t(across, across, highest)
        rest = rest - dot(basis, across, highest)
    inverse = eliminate(inner)
    basis = lax.dot_general(
        rest, inverse, (((1,), (1,)), ((), ())), preferred_element_type=f32, precision=highest
    )
    eye = iota(inverse.shape, 0) == iota(inverse.shape, 1)
    diagonal = jnp.sum(jnp.where(eye, inverse, f32(0.0)), axis=0, keepdims=True)
    return basis, (1.0 / diagonal) / scale_down


def piece_body(scale_down, mine_ref, other_ref, basis_ref, spectrum_ref, product_ref):
    product = joined_rows(mine_ref, other_ref, product_ref)
    basis_ref[...], spectrum_ref[...] = basis_piece(scale_down, product, [])


def first_piece(mine, other, scale_down):
    half, columns = mine.shape
    return pl.pallas_call(
        functools.partial(piece_body, scale_down),
        out_shape=(
            jax.ShapeDtypeStruct((2 * half, columns), f32),
            jax.ShapeDtypeStruct((1, columns), f32),
        ),
        scratch_shapes=[pltpu.VMEM((2 * half, columns), f32)],
        compiler_params=params(8),
        name="basis_first",
    )(mine, other)


def basis_body(scale_down, first_ref, first_spectrum_ref, mine_ref, other_ref, own_ref, part_ref, taps_ref,
               spectrum_ref, product_ref, wide_ref):
    half = mine_ref.shape[0]
    core = lax.axis_index("grp") % 2
    product = joined_rows(mine_ref, other_ref, product_ref)
    first = first_ref[...]
    wide_ref[0] = first
    wide_ref[1], spectrum_ref[:, LANES:] = basis_piece(scale_down, product, [first])
    spectrum_ref[:, :LANES] = first_spectrum_ref[...]
    own_ref[...] = jnp.concatenate([wide_ref[0], wide_ref[1]], axis=1).astype(bf16)
    part_ref[...] = own_ref[pl.ds(pl.multiple_of(core * half, half), half), :]
    at = 0
    taps, level = half, 1
    while at < taps_ref.shape[0]:
        rows = max(taps, LANES)
        chosen = jnp.concatenate(
            [wide_ref[part, pl.ds(0, taps, stride=2**level), :] for part in range(2)], axis=1
        )
        if rows > taps:
            chosen = jnp.concatenate([chosen, jnp.zeros((rows - taps, 2 * LANES), f32)], axis=0)
        taps_ref[at : at + rows, :] = chosen.astype(bf16)
        at, taps, level = at + rows, taps // 2, level + 1


def find_basis(mine, other, tap_rows, scale_down):
    first, first_spectrum = first_piece(mine[0], other[0], scale_down)
    half = mine[0].shape[0]
    length, rank = 2 * half, 2 * LANES
    return pl.pallas_call(
        functools.partial(basis_body, scale_down),
        out_shape=(
            jax.ShapeDtypeStruct((length, rank), bf16),
            jax.ShapeDtypeStruct((half, rank), bf16),
            jax.ShapeDtypeStruct((tap_rows, rank), bf16),
            jax.ShapeDtypeStruct((1, rank), f32),
        ),
        scratch_shapes=[pltpu.VMEM((length, LANES), f32), pltpu.VMEM((2, length, LANES), f32)],
        compiler_params=params(8),
        name="basis_second",
    )(first, first_spectrum, mine[1], other[1])


def level_sizes(levels, tap_count):
    return [max(1, (tap_count >> r) // LANES) for r in range(levels)]


def level_starts(total, levels):
    starts = [0]
    for r in range(levels):
        starts.append(starts[-1] + (total >> r))
    return starts


def levels_body(levels, detectors, history_ref, strain_ref, flipped_ref, level_ref):
    lead = history_ref.shape[1] // LANES
    each = lead + strain_ref.shape[1] // LANES
    total = detectors * each
    starts = level_starts(total, levels)
    source = iota((2 * LANES, 2 * LANES), 0)
    target = iota((2 * LANES, 2 * LANES), 1)
    even_odd = (source == 2 * (target % LANES) + target // LANES).astype(f32).astype(bf16)
    reverse = (
        iota((LANES, LANES), 0) + iota((LANES, LANES), 1) == LANES - 1
    ).astype(f32).astype(bf16)
    for d in range(detectors):
        for q in range(each):
            from_ref, at = (history_ref, q) if q < lead else (strain_ref, q - lead)
            level_ref[d * each + q : d * each + q + 1, :] = from_ref[
                d : d + 1, at * LANES : (at + 1) * LANES
            ]
    for r in range(levels):
        rows = total >> r
        at = starts[r]
        if r > 0:
            before = starts[r - 1]
            joined = jnp.concatenate(
                [
                    level_ref[pl.ds(before, rows, stride=2), :],
                    level_ref[pl.ds(before + 1, rows, stride=2), :],
                ],
                axis=1,
            )
            high, middle, low = split3(joined)
            both = (dot(high, even_odd) + dot(middle, even_odd)) + dot(low, even_odd)
            level_ref[at : at + rows, :] = (both[:, :LANES] + both[:, LANES:]) * inv_root_two
        rounded = level_ref[at : at + rows, :].astype(bf16)
        flipped_ref[at : at + rows, :] = dot(rounded, reverse)


def flipped_levels(history, strain, levels):
    detectors = strain.shape[0]
    total = detectors * (history.shape[1] + strain.shape[1]) // LANES
    held = -(-level_starts(total, levels)[-1] // SUBLANES) * SUBLANES
    return pl.pallas_call(
        functools.partial(levels_body, levels, detectors),
        out_shape=jax.ShapeDtypeStruct((held, LANES), f32),
        scratch_shapes=[pltpu.VMEM((held, LANES), f32)],
        compiler_params=params(6),
        name="strain_levels",
    )(history, strain)


def tiles_body(wanted, total, levels, blocks, detectors, chunks, flipped_ref, tiles_ref):
    step = pl.program_id(0)
    starts = level_starts(total, levels)
    detector = step // chunks
    chunk = step % chunks
    lower = iota((LANES, LANES), 1) <= iota((LANES, LANES), 0)
    at = 0
    for r in wanted:
        rows = (total >> r) // detectors
        history = (1 << (levels - 1)) >> r
        count = (rows - history) // chunks
        first = starts[r] + detector * rows + history + chunk * count - (blocks[r] - 1)

        def turned(row):
            line = jnp.broadcast_to(flipped_ref[pl.ds(row, 1), :], (LANES, LANES))
            return pltpu.roll(line, 1, 1, stride=1, stride_axis=0)

        before = turned(first - 1)
        for i in range(count + blocks[r] - 1):
            now = turned(first + i)
            tiles_ref[0, at] = jnp.where(lower, now, before).astype(bf16)
            before = now
            at += 1


def make_tiles(flipped, total, wanted, levels, blocks, detectors, chunks):
    count = 0
    for r in wanted:
        rows = (total >> r) // detectors
        lead = (1 << (levels - 1)) >> r
        count += (rows - lead) // chunks + blocks[r] - 1
    steps = detectors * chunks
    return pl.pallas_call(
        functools.partial(tiles_body, wanted, total, levels, blocks, detectors, chunks),
        grid=(steps,),
        out_shape=jax.ShapeDtypeStruct((steps, count, LANES, LANES), bf16),
        in_specs=[pl.BlockSpec(flipped.shape, lambda i: (0, 0))],
        out_specs=pl.BlockSpec((1, count, LANES, LANES), lambda i: (i, 0, 0, 0)),
        compiler_params=params(6),
        cost_estimate=pl.CostEstimate(
            flops=steps * count * LANES * LANES * 64,
            bytes_accessed=steps * count * LANES * LANES * 2, transcendentals=0,
        ),
        name="toeplitz_tiles",
    )(flipped)


def filter_body(blocks, chunks, tiles_ref, taps_ref, *refs):
    count = len(blocks)
    out_refs, held_refs = refs[:count], refs[count : 2 * count]
    here_ref, out_sem = tiles_ref, refs[2 * count]
    steps = tiles_ref.shape[0]

    def give(step, r):
        rows = out_refs[r].shape[2] // chunks
        spot = (step // chunks, pl.ds(step % chunks * rows, rows))
        return pltpu.make_async_copy(
            held_refs[r].at[spot], out_refs[r].at[(0, *spot)], out_sem.at[step, r]
        )

    def work(step):
        at, tap_at = 0, 0
        for r in range(count):
            rows = out_refs[r].shape[2] // chunks
            b = blocks[r]
            taps = taps_ref[tap_at : tap_at + b * LANES, :]
            group = min(rows, 512)
            for i in range(0, rows, group):
                first = at + b - 1 + i // LANES
                columns = [
                    here_ref[step, first - k : first - k + group // LANES].reshape(group, LANES)
                    for k in range(b)
                ]
                joined = jnp.concatenate(columns, axis=1) if b > 1 else columns[0]
                place = pl.ds(step % chunks * rows + i, group)
                held_refs[r][step // chunks, place, :] = dot(joined, taps).astype(bf16)
            give(step, r).start()
            at += rows // LANES + b - 1
            tap_at += b * LANES

    for step in range(steps):
        work(step)
    for step in range(steps):
        for r in range(count):
            give(step, r).wait()


def filter_levels(tiles, taps, lengths, blocks, detectors, chunks):
    rank = taps.shape[1]
    steps = tiles.shape[0]
    anywhere = pl.BlockSpec(memory_space=pl.ANY)
    return pl.pallas_call(
        functools.partial(filter_body, blocks, chunks),
        out_shape=[jax.ShapeDtypeStruct((1, detectors, n, rank), bf16) for n in lengths],
        in_specs=[pl.BlockSpec(memory_space=pltpu.VMEM)] * 2,
        out_specs=[anywhere] * len(lengths),
        scratch_shapes=[pltpu.VMEM((detectors, n, rank), bf16) for n in lengths]
        + [pltpu.SemaphoreType.DMA((steps, len(lengths)))],
        compiler_params=params(18),
        cost_estimate=pl.CostEstimate(
            flops=2 * sum(n * b for n, b in zip(lengths, blocks)) * LANES * rank * detectors,
            bytes_accessed=2 * detectors * sum(lengths) * rank + 2 * math.prod(tiles.shape),
            transcendentals=0,
        ),
        name="filter_levels",
    )(tiles, taps)


def mixing_body(bins, grp, owner_ref, white_ref, own_ref, mine_ref, other_ref, out_hbm, bases_ref, out_ref,
                sem):
    rows, width = white_ref.shape
    half = width // 2
    core, here = lax.axis_index("grp") % 2, lax.axis_index("bin")

    def place(row, count):
        return pl.ds(pl.multiple_of(row, count), count)

    bases_ref[:width] = own_ref[...]
    bases_ref[place((1 + core) * width, width), :] = mine_ref[:width]
    bases_ref[place((2 - core) * width, width), :] = other_ref[:width]
    bases_ref[place(3 * width + core * half, half), :] = mine_ref[width:]
    bases_ref[place(3 * width + (1 - core) * half, half), :] = other_ref[width:]
    mask = spread((owner_ref[...] // grp) ^ here, rows, bins, LANES).astype(bf16)
    pieces = 4
    piece = rows // pieces
    given = []
    for i in range(pieces):
        at = slice(i * piece, (i + 1) * piece)
        white = white_ref[at, :]
        masked = jnp.concatenate(
            [
                white * jnp.concatenate([mask[at, m * LANES : (m + 1) * LANES]] * (width // LANES), axis=1)
                for m in range(bins)
            ],
            axis=1,
        )
        out_ref[at, :] = dot(masked, bases_ref[...]).astype(bf16)
        rows_at = pl.ds(i * piece, piece)
        given.append(pltpu.make_async_copy(out_ref.at[rows_at], out_hbm.at[rows_at], sem.at[i]))
        given[-1].start()
    for copy in given:
        copy.wait()


def mix(owner, white, own, mine, other, bins, grp):
    rows, width = white.shape
    rank = own.shape[1]
    return pl.pallas_call(
        functools.partial(mixing_body, bins, grp),
        out_shape=jax.ShapeDtypeStruct((rows, rank), bf16),
        in_specs=[pl.BlockSpec(memory_space=pltpu.VMEM)] * 5,
        out_specs=pl.BlockSpec(memory_space=pl.ANY),
        scratch_shapes=[
            pltpu.VMEM((bins * width, rank), bf16),
            pltpu.VMEM((rows, rank), bf16),
            pltpu.SemaphoreType.DMA((4,)),
        ],
        compiler_params=params(14),
        name="mixing",
    )(owner, white, own, mine, other)


def local(templates, owner_device, rate_code, rate_gains, sketch, strain):
    rows, width = templates.shape
    grp = lax.axis_size("grp")
    bins = lax.axis_size("bin")
    levels = rate_gains.shape[0]
    detectors, samples = strain.shape
    owner = owner_device.reshape(1, rows)

    blocks = level_sizes(levels, width)
    chunks = 4
    reach = LANES << (levels - 1)
    total = detectors * (reach + samples) // LANES
    white, keep, send = front(
        owner, rate_code.reshape(1, rows), rate_gains, templates, sketch, bins, grp
    )

    def before(x, done):
        x, here = lax.optimization_barrier((x, strain))
        history = lax.ppermute(here[:, -reach:], "grp", [(i, i + 1) for i in range(grp - 1)])
        return x, (history,)

    def lines(x, done):
        return x, (flipped_levels(*done, strain, levels),)

    def tiles_of(wanted):
        def work(x, done):
            x, flipped, *rest = lax.optimization_barrier((x, *done))
            tiles = make_tiles(flipped, total, wanted, levels, blocks, detectors, chunks)
            return x, (flipped, *rest, tiles)

        return work

    mine, other, (_, tiles_coarse, tiles_fine) = reduce_products(
        keep, send, bins, grp, (before, lines, tiles_of(tuple(range(1, levels))), tiles_of((0,)))
    )
    own, part, taps, spectrum = find_basis(
        mine, other, sum(blocks[1:]) * LANES, rows * grp * math.sqrt(width)
    )
    near = flip_bin(own, (1, 2), bins, grp)
    far = flip_bin(part, (3, 3), bins, grp)
    lengths = [samples >> r for r in range(levels)]
    (finest,) = filter_levels(tiles_fine, own, lengths[:1], blocks[:1], detectors, chunks)
    near, far, finest = lax.optimization_barrier((near, far, finest))
    theirs = jnp.concatenate([near, far], axis=0)
    theirs_other = flip_core(theirs, grp)
    taps, theirs = lax.optimization_barrier((taps, theirs))
    filtered = filter_levels(tiles_coarse, taps, lengths[1:], blocks[1:], detectors, chunks)
    mixing = mix(owner, white, own, theirs, theirs_other, bins, grp)
    return (mixing, spectrum, finest, *filtered)


def solution(mesh):
    return jax.shard_map(
        local,
        mesh=mesh,
        in_specs=(
            P(("bin", "grp"), None),
            P(("bin", "grp"), None),
            P(("bin", "grp")),
            P(),
            P(),
            P(None, "grp"),
        ),
        out_specs=(
            P(("bin", "grp"), None),
            P("bin", None),
            P("bin", None, "grp", None),
            P("bin", None, "grp", None),
            P("bin", None, "grp", None),
            P("bin", None, "grp", None),
            P("bin", None, "grp", None),
        ),
        check_vma=False,
    )
```
